256 devices in a mesh: row: 8 (over z_lo, core), col: 16 (over y, x), depth: 2 (over z_hi).
Axes of the slice: x: 4, y: 4, z: 8 (z_hi: 2, z_lo: 4; z = z_hi * 4 + z_lo), core: 2. Of those that a mesh axis runs over, the one named last changes fastest.
Arguments:
- activations: bfloat16 [2048, 8192], P(('depth', 'col'), 'row'), may hold values from -6 to 6
- gate_weight: bfloat16 [8192, 16384], P('row', 'col'), may hold values from -0.0625 to 0.0625
- up_weight: bfloat16 [8192, 16384], P('row', 'col'), may hold values from -0.0625 to 0.0625
- down_weight: bfloat16 [16384, 8192], P('col', 'row'), may hold values from -0.046875 to 0.046875
- output_grad: bfloat16 [2048, 8192], P(('depth', 'col'), 'row'), may hold values from -6 to 6
Outputs:
- layer_out: bfloat16 [2048, 8192], P(('depth', 'col'), 'row')
- input_grad: bfloat16 [2048, 8192], P(('depth', 'col'), 'row')
- gate_weight_grad: bfloat16 [8192, 16384], P(('row', 'depth'), 'col')
- up_weight_grad: bfloat16 [8192, 16384], P(('row', 'depth'), 'col')
- down_weight_grad: bfloat16 [16384, 8192], P('col', ('row', 'depth'))
The draws below stay inside these ranges and needn't reach their ends.
All inputs are finite; a program needn't handle non-finite values.
Results may differ from the reference program's by a relative error of at most 0.019.
Values may be sent and summed in bfloat16 or wider, within the bound.
No kernel may reach another device: no remote copies, remote signals or barrier semaphores. Data moves between devices by JAX's collectives and lax.ppermute only.
A program may use at most 128 MiB of HBM per device.

```python
import jax
import jax.numpy as jnp

D = 8192
FF = 16384
TOKENS = 2048


def steps_of(key, extent, cuts, low, top_value):
    gain, own = 1.0, jax.random.fold_in(key, 6)
    for dim, blocks in cuts:
        heights = jnp.exp(jax.random.uniform(jax.random.fold_in(own, dim), (blocks,), jnp.float32, low / len(cuts), top_value / len(cuts)))
        gain = gain * jnp.repeat(heights, extent[dim] // blocks).reshape([-1 if axis == dim else 1 for axis in range(len(extent))])
    return gain


def scatter_about(key, extent, scale, bound, cuts=(), dtype=jnp.bfloat16):
    drawn = jax.random.normal(key, extent, jnp.float32) * scale
    if len(cuts) > 0:
        drawn = steps_of(key, extent, cuts, -0.22, 0.18) * drawn
    return jnp.clip(drawn, min=-bound, max=bound).astype(dtype)


def setup_inputs(seed: int = 0) -> dict:
    key_of = jax.random.split(jax.random.key(seed), 6)
    return {
        "activations": scatter_about(key_of[0], (TOKENS, D), 1.0, 6.0, ((0, 32), (1, 8))),
        "gate_weight": scatter_about(key_of[1], (D, FF), D ** -0.5, 0.0625, ((0, 8), (1, 16))),
        "up_weight": scatter_about(key_of[2], (D, FF), D ** -0.5, 0.0625, ((0, 8), (1, 16))),
        "down_weight": scatter_about(key_of[3], (FF, D), FF ** -0.5, 0.046875, ((0, 16), (1, 8))),
        "output_grad": scatter_about(key_of[4], (TOKENS, D), 1.0, 6.0, ((0, 32), (1, 8))),
    }


def reference(activations, gate_weight, up_weight, down_weight, output_grad):
    gate_sums = jnp.dot(activations, gate_weight, preferred_element_type=jnp.float32)
    up_sums = jnp.dot(activations, up_weight, preferred_element_type=jnp.float32)
    sigmoid_gate = jax.nn.sigmoid(gate_sums)
    activated = gate_sums * sigmoid_gate
    hidden = (activated * up_sums).astype(jnp.bfloat16)
    layer_out = jnp.dot(hidden, down_weight, preferred_element_type=jnp.float32).astype(jnp.bfloat16)
    hidden_grad = jnp.dot(output_grad, down_weight.T, preferred_element_type=jnp.float32)
    gate_grad = (hidden_grad * up_sums * sigmoid_gate * (1.0 + gate_sums * (1.0 - sigmoid_gate))).astype(jnp.bfloat16)
    up_grad = (hidden_grad * activated).astype(jnp.bfloat16)
    input_grad = (jnp.dot(gate_grad, gate_weight.T, preferred_element_type=jnp.float32)
                  + jnp.dot(up_grad, up_weight.T, preferred_element_type=jnp.float32)).astype(jnp.bfloat16)
    gate_weight_grad = jnp.dot(activations.T, gate_grad, preferred_element_type=jnp.float32).astype(jnp.bfloat16)
    up_weight_grad = jnp.dot(activations.T, up_grad, preferred_element_type=jnp.float32).astype(jnp.bfloat16)
    down_weight_grad = jnp.dot(hidden.T, output_grad, preferred_element_type=jnp.float32).astype(jnp.bfloat16)
    return (layer_out, input_grad, gate_weight_grad, up_weight_grad, down_weight_grad)
```

```python
import jax
import jax.numpy as jnp
from jax import lax
from jax.sharding import PartitionSpec as P

AXES = ("row", "col", "depth")
LAST = (((1,), (1,)), ((), ()))
FIRST = (((0,), (0,)), ((), ()))
F32 = jnp.float32
BF16 = jnp.bfloat16


def send(value, dx=0, dy=0, dz=0, flip=0):
    pairs = []
    for i in range(256):
        row, col, depth = i // 32, i // 2 % 16, i % 2
        z = (depth * 4 + row // 2 + dz) % 8
        core = row % 2 ^ flip
        y, x = (col // 4 + dy) % 4, (col % 4 + dx) % 4
        pairs.append((i, ((z % 4 * 2 + core) * 16 + y * 4 + x) * 2 + z // 4))
    return lax.ppermute(value, AXES, pairs)


def step(value, axis, by):
    return send(value, **{axis: by})


def gather_ring(value, axis):
    half = value.shape[0] // 2
    before = step(value, axis, 1)
    after = step(value, axis, -1)
    low = step(before[:half], axis, 1)
    high = step(after[half:], axis, -1)
    return [value, after, jnp.concatenate([low, high]), before]


def gather_plane(value, axes):
    lines = jnp.stack(gather_ring(value, axes[0]))
    whole = jnp.stack(gather_ring(lines, axes[1]))
    return whole if axes[0] == "dx" else jnp.swapaxes(whole, 0, 1)


def scatter_ring(blocks, axis):
    here, after, far, before = [block.astype(F32) for block in blocks]
    half = here.shape[0] // 2
    up = step(far[:half].astype(BF16), axis, 1).astype(F32)
    down = step(far[half:].astype(BF16), axis, -1).astype(F32)
    after = jnp.concatenate([after[:half] + up, after[half:]]).astype(BF16)
    before = jnp.concatenate([before[:half], before[half:] + down]).astype(BF16)
    return here + step(after, axis, 1).astype(F32) + step(before, axis, -1).astype(F32)


def scatter_plane(value, axes):
    place = 1 if axes[0] == "dy" else 2
    lines = scatter_ring([jnp.take(value, j, axis=place) for j in range(4)], axes[0])
    return scatter_ring([lines[:, j] for j in range(4)], axes[1])


def dot(a, b, dims=(((1,), (0,)), ((), ()))):
    return lax.dot_general(a, b, dims, preferred_element_type=F32)


def half_of(value, which, axis):
    size = value.shape[axis] // 2
    return lax.dynamic_slice_in_dim(value, which * size, size, axis)


def pick(value, index, axis):
    return lax.dynamic_index_in_dim(value, index, axis, keepdims=False)


def local(activations, gate_weight, up_weight, down_weight, output_grad):
    tokens, feats = activations.shape
    units = gate_weight.shape[1]
    group = tokens // 8
    rows = 16 * group
    hu = units // 2
    row = lax.axis_index("row")
    line, core = row // 2, row % 2
    depth = lax.axis_index("depth")

    own_in = jnp.concatenate([half_of(gate_weight, core, 1), half_of(up_weight, core, 1)], axis=1)
    own_down = half_of(down_weight, core, 0)
    sib_in = send(
        jnp.concatenate([half_of(gate_weight, 1 - core, 1), half_of(up_weight, 1 - core, 1)], axis=1), flip=1
    )
    sib_down = send(half_of(down_weight, 1 - core, 0), flip=1)

    pair = jnp.stack([activations, output_grad]).reshape(2, 8, group, feats)
    foreign = send(lax.dynamic_slice_in_dim(pair[:, 1:7], line, 3, 1), dz=4)
    chosen = []
    for s in range(4):
        right = pick(pair, jnp.maximum(line - s, 0), 1)
        left = pick(pair, jnp.minimum(4 + line + s, 7), 1)
        if s > 0:
            right = jnp.where(line >= s, right, foreign[:, 3 - s])
            left = jnp.where(line + s <= 3, left, foreign[:, s - 1])
        chosen.append(jnp.stack([right, left], axis=1))
    chosen = jnp.stack(chosen, axis=1)
    others = send(half_of(chosen, 1 - depth, 4), dz=4)

    def panel(value, axes):
        whole = gather_plane(value, axes)
        return jnp.transpose(whole, (2, 3, 0, 1, 4, 5)).reshape(4, 2 * rows, value.shape[-1])

    act = panel(chosen[0], ("dx", "dy"))
    cot = panel(chosen[1], ("dy", "dx"))
    act_sib = [send(act[0], flip=1), send(act[1:], flip=1)]
    cot_sib = [send(cot[0], flip=1), send(cot[1:], flip=1)]

    def partial(s):
        a2 = act_sib[0] if s == 0 else act_sib[1][s - 1]
        c2 = cot_sib[0] if s == 0 else cot_sib[1][s - 1]
        first = dot(act[s], own_in) + dot(a2, sib_in)
        second = dot(cot[s], own_down, LAST) + dot(c2, sib_down, LAST)
        return jnp.concatenate([first, second], axis=1)

    sums = partial(0)
    for s in range(1, 4):
        message = sums.astype(BF16)
        right = send(message[:rows], dz=1)
        left = send(message[rows:], dz=-1)
        sums = partial(s) + jnp.concatenate([right, left]).astype(F32)

    gate_sums, up_sums, hidden_grad = sums[:, :hu], sums[:, hu : 2 * hu], sums[:, 2 * hu :]
    sigmoid_gate = jax.nn.sigmoid(gate_sums)
    activated = gate_sums * sigmoid_gate
    hidden = (activated * up_sums).astype(BF16)
    gate_grad = (
        hidden_grad * up_sums * sigmoid_gate * (1.0 + gate_sums * (1.0 - sigmoid_gate))
    ).astype(BF16)
    up_grad = (hidden_grad * activated).astype(BF16)

    chunk = {0: jnp.stack([t.reshape(2, rows, hu) for t in (hidden, gate_grad, up_grad)], axis=1)}
    for j in range(1, 4):
        chunk[-j] = send(chunk[1 - j], dz=1)
        chunk[j] = send(chunk[j - 1], dz=-1)
    part = {(j, side): chunk[j][side] for j in range(-3, 4) for side in (0, 1)}
    far_right = send(chunk[-3][0], dz=1)
    far_left = send(chunk[3][1], dz=-1)
    part[-4, 0], part[4, 1] = far_right, far_left
    sibling = {j: send(chunk[j], flip=1) for j in range(-3, 4)}
    sib_part = {(j, side): sibling[j][side] for j in range(-3, 4) for side in (0, 1)}
    sib_part[-4, 0], sib_part[4, 1] = send(far_right, flip=1), send(far_left, flip=1)

    def lay(keys):
        mine = jnp.concatenate([part[key] for key in keys], axis=1)
        theirs = jnp.concatenate([sib_part[key] for key in keys], axis=1)
        return jnp.where(
            core == 0,
            jnp.concatenate([mine, theirs], axis=2),
            jnp.concatenate([theirs, mine], axis=2),
        )

    def outputs(keys):
        whole = lay(keys)
        shape = (len(keys), 4, 4, group, feats)
        layer = dot(whole[0], down_weight)
        inputs = dot(whole[1], gate_weight, LAST) + dot(whole[2], up_weight, LAST)
        layer = scatter_plane(layer.astype(BF16).reshape(shape), ("dy", "dx"))
        inputs = scatter_plane(inputs.astype(BF16).reshape(shape), ("dx", "dy"))
        return jnp.stack([layer, inputs]).astype(BF16)

    near = outputs([(-1, 0), (0, 0), (1, 0), (-1, 1), (0, 1), (1, 1)])
    next_near = outputs([(2, 0), (-2, 1)])
    rights = jnp.concatenate([near[:, :3], next_near[:, :1]], axis=1)
    lefts = jnp.concatenate([next_near[:, 1:], near[:, 3:]], axis=1)
    away = lax.dynamic_slice_in_dim(jnp.concatenate([lefts, rights], axis=1), 3 - line, 5, 1)
    back = send(away, dz=4)
    result = []
    for j in range(4):
        result.append(jnp.where(line <= j, back[:, j + 1], pick(rights, jnp.minimum(j - line + 4, 3), 1)))
    for j in range(4):
        result.append(jnp.where(line >= j, back[:, j], pick(lefts, jnp.maximum(j - line - 1, 0), 1)))
    result = jnp.stack(result, axis=1).reshape(2, tokens, feats)

    act_half, cot_half = half_of(act, depth, 2), half_of(cot, depth, 2)
    act_other = panel(others[0], ("dx", "dy"))
    cot_other = panel(others[1], ("dy", "dx"))
    hf = feats // 2

    def join(mine, theirs):
        return jnp.concatenate([mine.reshape(-1, hf), theirs.reshape(-1, hf)])

    early = lay(
        [key for s in (1, 2, 3) for key in ((3 - s, 0), (s - 3, 1))]
        + [key for s in (0, 1) for key in ((-1 - s, 0), (1 + s, 1))]
    )
    late = lay([(3, 0), (-3, 1)] + [key for s in (2, 3) for key in ((-1 - s, 0), (1 + s, 1))])
    act_early, act_late = join(act_half[1:], act_other[:2]), join(act_half[:1], act_other[2:])
    cot_early, cot_late = join(cot_half[1:], cot_other[:2]), join(cot_half[:1], cot_other[2:])
    gate_total = dot(act_early, early[1], FIRST) + dot(act_late, late[1], FIRST)
    up_total = dot(act_early, early[2], FIRST) + dot(act_late, late[2], FIRST)
    down_total = dot(early[0], cot_early, FIRST) + dot(late[0], cot_late, FIRST)
    return (
        result[0],
        result[1],
        gate_total.astype(BF16),
        up_total.astype(BF16),
        down_total.astype(BF16),
    )


def solution(mesh):
    return jax.shard_map(
        local,
        mesh=mesh,
        in_specs=(
            P(("depth", "col"), "row"),
            P("row", "col"),
            P("row", "col"),
            P("col", "row"),
            P(("depth", "col"), "row"),
        ),
        out_specs=(
            P(("depth", "col"), "row"),
            P(("depth", "col"), "row"),
            P(("row", "depth"), "col"),
            P(("row", "depth"), "col"),
            P("col", ("row", "depth")),
        ),
        check_vma=False,
    )
```

```python
import jax
import jax.numpy as jnp
from jax import lax
from jax.sharding import PartitionSpec as P

AXES = ("row", "col", "depth")
LAST = (((1,), (1,)), ((), ()))
FIRST = (((0,), (0,)), ((), ()))
F32 = jnp.float32
BF16 = jnp.bfloat16


def send(value, dx=0, dy=0, dz=0, flip=0):
    pairs = []
    for i in range(256):
        row, col, depth = i // 32, i // 2 % 16, i % 2
        z = (depth * 4 + row // 2 + dz) % 8
        core = row % 2 ^ flip
        y, x = (col // 4 + dy) % 4, (col % 4 + dx) % 4
        pairs.append((i, ((z % 4 * 2 + core) * 16 + y * 4 + x) * 2 + z // 4))
    return lax.ppermute(value, AXES, pairs)


def step(value, axis, by):
    return send(value, **{axis: by})


def behind(value, *done):
    return lax.optimization_barrier((value, *done))[0]


def gather_ring(value, axis):
    half = value.shape[0] // 2
    before = step(value, axis, 1)
    after = step(value, axis, -1)
    low = step(before[:half], axis, 1)
    high = step(after[half:], axis, -1)
    return [value, after, jnp.concatenate([low, high]), before]


def gather_line(value, axis):
    far = step(value, axis, 2)
    return jnp.stack([value, step(value, axis, -1), far, step(value, axis, 1)])


def gather_plane(value, axes, done):
    lines = behind(gather_line(value, axes[0]), *done)
    whole = jnp.stack(gather_ring(lines, axes[1]))
    return whole if axes[0] == "dx" else jnp.swapaxes(whole, 0, 1)


def scatter_ring(blocks, axis, done):
    here, after, far, before = blocks
    half = here.shape[0] // 2
    up = step(far[:half].astype(BF16), axis, 1).astype(F32)
    down = step(far[half:].astype(BF16), axis, -1).astype(F32)
    after = jnp.concatenate([after[:half].astype(F32) + up, after[half:].astype(F32)]).astype(BF16)
    before = jnp.concatenate([before[:half].astype(F32), before[half:].astype(F32) + down]).astype(BF16)
    after, before = behind(after, *done), behind(before, *done)
    return here.astype(F32) + step(after, axis, 1).astype(F32) + step(before, axis, -1).astype(F32)


def scatter_line(blocks, axis):
    here, after, far, before = blocks
    total = here + step(after.astype(BF16), axis, 1).astype(F32)
    total = total + step(before.astype(BF16), axis, -1).astype(F32)
    return total + step(far.astype(BF16), axis, 2).astype(F32)


def scatter_plane(value, axes, done, done_late):
    place = 1 if axes[0] == "dy" else 2
    lines = scatter_ring([jnp.take(value, j, axis=place) for j in range(4)], axes[0], done)
    lines = behind(lines, *done_late)
    return scatter_line([lines[:, j] for j in range(4)], axes[1])


def dot(a, b, dims=(((1,), (0,)), ((), ()))):
    return lax.dot_general(a, b, dims, preferred_element_type=F32)


def half_of(value, which, axis):
    size = value.shape[axis] // 2
    return lax.dynamic_slice_in_dim(value, which * size, size, axis)


def pick(value, index, axis):
    return lax.dynamic_index_in_dim(value, index, axis, keepdims=False)


def local(activations, gate_weight, up_weight, down_weight, output_grad):
    tokens, feats = activations.shape
    units = gate_weight.shape[1]
    group = tokens // 8
    rows = 16 * group
    hu = units // 2
    row = lax.axis_index("row")
    line, core = row // 2, row % 2
    depth = lax.axis_index("depth")

    own_in = jnp.concatenate([half_of(gate_weight, core, 1), half_of(up_weight, core, 1)], axis=1)
    own_down = half_of(down_weight, core, 0)
    sib_in = send(
        jnp.concatenate([half_of(gate_weight, 1 - core, 1), half_of(up_weight, 1 - core, 1)], axis=1), flip=1
    )
    sib_down = send(half_of(down_weight, 1 - core, 0), flip=1)

    pair = jnp.stack([activations, output_grad]).reshape(2, 8, group, feats)
    foreign = send(lax.dynamic_slice_in_dim(pair[:, 1:7], line, 3, 1), dz=4)
    chosen = []
    for s in range(4):
        right = pick(pair, jnp.maximum(line - s, 0), 1)
        left = pick(pair, jnp.minimum(4 + line + s, 7), 1)
        if s > 0:
            right = jnp.where(line >= s, right, foreign[:, 3 - s])
            left = jnp.where(line + s <= 3, left, foreign[:, s - 1])
        chosen.append(jnp.stack([right, left], axis=1))
    chosen = jnp.stack(chosen, axis=1)
    others = send(half_of(chosen, 1 - depth, 4), dz=4)
    others = lax.all_gather(others, "col").reshape(4, 4, 2, 4, 2, group, feats // 2)
    col = lax.axis_index("col")
    for axis, at in ((0, col // 4), (1, col % 4)):
        others = lax.dynamic_slice_in_dim(jnp.concatenate([others, others], axis=axis), at, 4, axis)
    others = jnp.transpose(others, (2, 3, 4, 0, 1, 5, 6)).reshape(2, 4, 2 * rows, feats // 2)

    def panel(value, axes):
        whole = gather_plane(value, axes, (sib_in, sib_down))
        return jnp.transpose(whole, (2, 3, 0, 1, 4, 5)).reshape(4, 2 * rows, value.shape[-1])

    act = panel(chosen[0], ("dx", "dy"))
    cot = panel(chosen[1], ("dy", "dx"))
    act_sib = [send(act[0], flip=1), send(act[1:], flip=1)]
    cot_sib = [send(cot[0], flip=1), send(cot[1:], flip=1)]

    def partial(s):
        a2 = act_sib[0] if s == 0 else act_sib[1][s - 1]
        c2 = cot_sib[0] if s == 0 else cot_sib[1][s - 1]
        first = dot(act[s], own_in) + dot(a2, sib_in)
        second = dot(cot[s], own_down, LAST) + dot(c2, sib_down, LAST)
        return jnp.concatenate([first, second], axis=1)

    sums = partial(0)
    for s in range(1, 4):
        message = sums.astype(BF16)
        right = send(message[:rows], dz=1)
        left = send(message[rows:], dz=-1)
        sums = partial(s) + jnp.concatenate([right, left]).astype(F32)

    gate_sums, up_sums, hidden_grad = sums[:, :hu], sums[:, hu : 2 * hu], sums[:, 2 * hu :]
    sigmoid_gate = jax.nn.sigmoid(gate_sums)
    activated = gate_sums * sigmoid_gate
    hidden = (activated * up_sums).astype(BF16)
    gate_grad = (
        hidden_grad * up_sums * sigmoid_gate * (1.0 + gate_sums * (1.0 - sigmoid_gate))
    ).astype(BF16)
    up_grad = (hidden_grad * activated).astype(BF16)

    chunk = {0: jnp.stack([t.reshape(2, rows, hu) for t in (hidden, gate_grad, up_grad)], axis=1)}
    for j in range(1, 4):
        chunk[-j] = send(chunk[1 - j], dz=1)
        chunk[j] = send(chunk[j - 1], dz=-1)
    part = {(j, side): chunk[j][side] for j in range(-3, 4) for side in (0, 1)}
    far_right = send(chunk[-3][0], dz=1)
    far_left = send(chunk[3][1], dz=-1)
    part[-4, 0], part[4, 1] = far_right, far_left
    sibling = {j: send(chunk[j], flip=1) for j in range(-3, 4)}
    sib_part = {(j, side): sibling[j][side] for j in range(-3, 4) for side in (0, 1)}
    sib_part[-4, 0], sib_part[4, 1] = send(far_right, flip=1), send(far_left, flip=1)

    def lay(keys):
        mine = jnp.concatenate([part[key] for key in keys], axis=1)
        theirs = jnp.concatenate([sib_part[key] for key in keys], axis=1)
        return jnp.where(
            core == 0,
            jnp.concatenate([mine, theirs], axis=2),
            jnp.concatenate([theirs, mine], axis=2),
        )

    def outputs(keys):
        whole = lay(keys)
        shape = (len(keys), 4, 4, group, feats)
        layer = dot(whole[0], down_weight)
        inputs = dot(whole[1], gate_weight, LAST) + dot(whole[2], up_weight, LAST)
        done, done_late = (chunk[-3], chunk[3]), (far_right, far_left)
        layer = scatter_plane(layer.astype(BF16).reshape(shape), ("dy", "dx"), done, done_late)
        inputs = scatter_plane(inputs.astype(BF16).reshape(shape), ("dx", "dy"), done, done_late)
        return jnp.stack([layer, inputs]).astype(BF16)

    near = outputs([(-1, 0), (0, 0), (1, 0), (2, 0), (-2, 1), (-1, 1), (0, 1), (1, 1)])
    rights, lefts = near[:, :4], near[:, 4:]
    away = lax.dynamic_slice_in_dim(jnp.concatenate([lefts, rights], axis=1), 3 - line, 5, 1)
    back = send(away, dz=4)
    result = []
    for j in range(4):
        result.append(jnp.where(line <= j, back[:, j + 1], pick(rights, jnp.minimum(j - line + 4, 3), 1)))
    for j in range(4):
        result.append(jnp.where(line >= j, back[:, j], pick(lefts, jnp.maximum(j - line - 1, 0), 1)))
    result = jnp.stack(result, axis=1).reshape(2, tokens, feats)

    act_half, cot_half = half_of(act, depth, 2), half_of(cot, depth, 2)
    act_other, cot_other = others[0], others[1]
    hf = feats // 2

    def join(mine, theirs):
        return jnp.concatenate([mine.reshape(-1, hf), theirs.reshape(-1, hf)])

    early = lay(
        [key for s in (1, 2, 3) for key in ((3 - s, 0), (s - 3, 1))]
        + [key for s in (0, 1) for key in ((-1 - s, 0), (1 + s, 1))]
    )
    late = lay([(3, 0), (-3, 1)] + [key for s in (2, 3) for key in ((-1 - s, 0), (1 + s, 1))])
    act_early, act_late = join(act_half[1:], act_other[:2]), join(act_half[:1], act_other[2:])
    cot_early, cot_late = join(cot_half[1:], cot_other[:2]), join(cot_half[:1], cot_other[2:])
    gate_total = dot(act_early, early[1], FIRST) + dot(act_late, late[1], FIRST)
    up_total = dot(act_early, early[2], FIRST) + dot(act_late, late[2], FIRST)
    down_total = dot(early[0], cot_early, FIRST) + dot(late[0], cot_late, FIRST)
    return (
        result[0],
        result[1],
        gate_total.astype(BF16),
        up_total.astype(BF16),
        down_total.astype(BF16),
    )


def solution(mesh):
    return jax.shard_map(
        local,
        mesh=mesh,
        in_specs=(
            P(("depth", "col"), "row"),
            P("row", "col"),
            P("row", "col"),
            P("col", "row"),
            P(("depth", "col"), "row"),
        ),
        out_specs=(
            P(("depth", "col"), "row"),
            P(("depth", "col"), "row"),
            P(("row", "depth"), "col"),
            P(("row", "depth"), "col"),
            P("col", ("row", "depth")),
        ),
        check_vma=False,
    )
```

```python
import jax
import jax.numpy as jnp
from jax import lax
from jax.sharding import PartitionSpec as P

AXES = ("row", "col", "depth")
LAST = (((1,), (1,)), ((), ()))
FIRST = (((0,), (0,)), ((), ()))
F32 = jnp.float32
BF16 = jnp.bfloat16


def send(value, dx=0, dy=0, dz=0, flip=0):
    pairs = []
    for i in range(256):
        row, col, depth = i // 32, i // 2 % 16, i % 2
        z = (depth * 4 + row // 2 + dz) % 8
        core = row % 2 ^ flip
        y, x = (col // 4 + dy) % 4, (col % 4 + dx) % 4
        pairs.append((i, ((z % 4 * 2 + core) * 16 + y * 4 + x) * 2 + z // 4))
    return lax.ppermute(value, AXES, pairs)


def step(value, axis, by):
    return send(value, **{axis: by})


def behind(value, *done):
    return lax.optimization_barrier((value, *done))[0]


def gather_ring(value, axis):
    half = value.shape[0] // 2
    before = step(value, axis, 1)
    after = step(value, axis, -1)
    low = step(before[:half], axis, 1)
    high = step(after[half:], axis, -1)
    return [value, after, jnp.concatenate([low, high]), before]


def gather_line(value, axis):
    far = step(value, axis, 2)
    return jnp.stack([value, step(value, axis, -1), far, step(value, axis, 1)])


def scatter_ring(blocks, axis, done):
    here, after, far, before = blocks
    half = here.shape[0] // 2
    up = step(far[:half].astype(BF16), axis, 1).astype(F32)
    down = step(far[half:].astype(BF16), axis, -1).astype(F32)
    after = jnp.concatenate([after[:half].astype(F32) + up, after[half:].astype(F32)]).astype(BF16)
    before = jnp.concatenate([before[:half].astype(F32), before[half:].astype(F32) + down]).astype(BF16)
    after, before = behind(after, *done), behind(before, *done)
    return here.astype(F32) + step(after, axis, 1).astype(F32) + step(before, axis, -1).astype(F32)


def scatter_line(blocks, axis):
    here, after, far, before = blocks
    total = here + step(after.astype(BF16), axis, 1).astype(F32)
    total = total + step(before.astype(BF16), axis, -1).astype(F32)
    return total + step(far.astype(BF16), axis, 2).astype(F32)


def scatter_plane(value, axes, done, done_late):
    place = 1 if axes[0] == "dy" else 2
    lines = scatter_ring([jnp.take(value, j, axis=place) for j in range(4)], axes[0], done)
    lines = behind(lines, *done_late)
    return scatter_line([lines[:, j] for j in range(4)], axes[1])


def dot(a, b, dims=(((1,), (0,)), ((), ()))):
    return lax.dot_general(a, b, dims, preferred_element_type=F32)


def half_of(value, which, axis):
    size = value.shape[axis] // 2
    return lax.dynamic_slice_in_dim(value, which * size, size, axis)


def pick(value, index, axis):
    return lax.dynamic_index_in_dim(value, index, axis, keepdims=False)


def local(activations, gate_weight, up_weight, down_weight, output_grad):
    tokens, feats = activations.shape
    units = gate_weight.shape[1]
    group = tokens // 8
    rows = 16 * group
    hu = units // 2
    row = lax.axis_index("row")
    line, core = row // 2, row % 2
    depth = lax.axis_index("depth")

    pair = jnp.stack([activations, output_grad]).reshape(2, 8, group, feats)
    foreign = send(lax.dynamic_slice_in_dim(pair[:, 1:7], line, 3, 1), dz=4)
    chosen = []
    for s in range(4):
        right = pick(pair, jnp.maximum(line - s, 0), 1)
        left = pick(pair, jnp.minimum(4 + line + s, 7), 1)
        if s > 0:
            right = jnp.where(line >= s, right, foreign[:, 3 - s])
            left = jnp.where(line + s <= 3, left, foreign[:, s - 1])
        chosen.append(jnp.stack([right, left], axis=1))
    chosen = jnp.stack(chosen, axis=1)
    lines = lax.optimization_barrier((gather_line(chosen[0], "dx"), gather_line(chosen[1], "dy")))
    act = jnp.stack(gather_ring(lines[0], "dy"))
    cot = jnp.swapaxes(jnp.stack(gather_ring(lines[1], "dx")), 0, 1)
    act = jnp.transpose(act, (2, 3, 0, 1, 4, 5)).reshape(4, 2 * rows, feats)
    cot = jnp.transpose(cot, (2, 3, 0, 1, 4, 5)).reshape(4, 2 * rows, feats)

    gate_late, up_late, down_late = behind((gate_weight, up_weight, down_weight), lines)
    own_in = jnp.concatenate([half_of(gate_late, core, 1), half_of(up_late, core, 1)], axis=1)
    own_down = half_of(down_late, core, 0)
    sib = jnp.concatenate([half_of(gate_late, 1 - core, 1), half_of(up_late, 1 - core, 1)], axis=1)
    sib = send(jnp.concatenate([sib, half_of(down_late, 1 - core, 0)]), flip=1)
    sib_in, sib_down = sib[:feats], sib[feats:]

    others = send(behind(half_of(chosen, 1 - depth, 4), lines), dz=4)
    act_sib = [send(act[0], flip=1), send(act[1:], flip=1)]
    cot_sib = [send(cot[0], flip=1), send(cot[1:], flip=1)]

    def partial(a, c, a2, c2):
        first = dot(a, own_in) + dot(a2, sib_in)
        second = dot(c, own_down, LAST) + dot(c2, sib_down, LAST)
        return jnp.concatenate([first, second], axis=1)

    sums = partial(act[0], cot[0], act_sib[0], cot_sib[0])
    message = sums.astype(BF16)
    others = gather_line(behind(others, message), "dx")
    others = jnp.stack(gather_ring(others, "dy"))
    others = jnp.transpose(others, (2, 3, 4, 0, 1, 5, 6)).reshape(2, 4, 2 * rows, feats // 2)
    act_rest, cot_rest = behind((act[1:], cot[1:]), message)
    for s in range(1, 4):
        right = send(message[:rows], dz=1)
        left = send(message[rows:], dz=-1)
        sums = partial(act_rest[s - 1], cot_rest[s - 1], act_sib[1][s - 1], cot_sib[1][s - 1])
        sums = sums + jnp.concatenate([right, left]).astype(F32)
        message = sums.astype(BF16)

    gate_sums, up_sums, hidden_grad = sums[:, :hu], sums[:, hu : 2 * hu], sums[:, 2 * hu :]
    sigmoid_gate = jax.nn.sigmoid(gate_sums)
    activated = gate_sums * sigmoid_gate
    hidden = (activated * up_sums).astype(BF16)
    gate_grad = (
        hidden_grad * up_sums * sigmoid_gate * (1.0 + gate_sums * (1.0 - sigmoid_gate))
    ).astype(BF16)
    up_grad = (hidden_grad * activated).astype(BF16)

    def sides(j, value):
        part[j, 0], part[j, 1] = value[:, :rows], value[:, rows:]

    def exchange(j, value):
        theirs = send(value, flip=1)
        sib_part[j, 0], sib_part[j, 1] = theirs[:, :rows], theirs[:, rows:]
        return theirs

    part, sib_part = {}, {}
    chunk = jnp.stack([hidden, gate_grad, up_grad])
    before, after = send(chunk, dz=1), send(chunk, dz=-1)
    near = [exchange(0, chunk), exchange(-1, before), exchange(1, after)]
    sides(0, chunk), sides(-1, before), sides(1, after)

    def onward(key_right, key_left, done):
        for (j, side), by in ((key_right, 1), (key_left, -1)):
            part[j, side] = send(behind(part[j + by, side], *done), dz=by)

    def onward_sib(*keys):
        for key in keys:
            sib_part[key] = send(part[key], flip=1)
        return [sib_part[key] for key in keys]

    onward((-2, 1), (2, 0), ())
    second = onward_sib((-2, 1), (2, 0))
    onward((-2, 0), (2, 1), [part[-2, 1], part[2, 0], *near])
    third = onward_sib((-2, 0), (2, 1))
    onward((-3, 1), (3, 0), [part[-2, 0], part[2, 1], *second])
    fourth = onward_sib((-3, 1), (3, 0))
    onward((-3, 0), (3, 1), [part[-3, 1], part[3, 0], *third])
    fifth = onward_sib((-3, 0), (3, 1))
    onward((-4, 0), (4, 1), [*fourth])
    onward_sib((-4, 0), (4, 1))

    def lay(keys):
        mine = jnp.concatenate([part[key] for key in keys], axis=1)
        theirs = jnp.concatenate([sib_part[key] for key in keys], axis=1)
        return jnp.where(
            core == 0,
            jnp.concatenate([mine, theirs], axis=2),
            jnp.concatenate([theirs, mine], axis=2),
        )

    def outputs(keys):
        whole = lay(keys)
        shape = (len(keys), 4, 4, group, feats)
        layer = dot(whole[0], down_weight)
        inputs = dot(whole[1], gate_weight, LAST) + dot(whole[2], up_weight, LAST)
        done, done_late = (part[-2, 0], part[2, 1]), (part[-3, 0], part[3, 1])
        layer = scatter_plane(layer.astype(BF16).reshape(shape), ("dy", "dx"), done, done_late)
        inputs = scatter_plane(inputs.astype(BF16).reshape(shape), ("dx", "dy"), done, done_late)
        return jnp.stack([layer, inputs]).astype(BF16)

    both = outputs([(-1, 0), (0, 0), (1, 0), (2, 0), (-2, 1), (-1, 1), (0, 1), (1, 1)])
    rights, lefts = both[:, :4], both[:, 4:]
    away = lax.dynamic_slice_in_dim(jnp.concatenate([lefts, rights], axis=1), 3 - line, 5, 1)
    back = send(behind(away, part[-4, 0], part[4, 1]), dz=4)
    result = []
    for j in range(4):
        result.append(jnp.where(line <= j, back[:, j + 1], pick(rights, jnp.minimum(j - line + 4, 3), 1)))
    for j in range(4):
        result.append(jnp.where(line >= j, back[:, j], pick(lefts, jnp.maximum(j - line - 1, 0), 1)))
    result = jnp.stack(result, axis=1).reshape(2, tokens, feats)

    act_half, cot_half = half_of(act, depth, 2), half_of(cot, depth, 2)
    act_other, cot_other = others[0], others[1]
    hf = feats // 2

    def join(mine, theirs):
        return jnp.concatenate([mine.reshape(-1, hf), theirs.reshape(-1, hf)])

    early = lay(
        [key for s in (1, 2, 3) for key in ((3 - s, 0), (s - 3, 1))]
        + [key for s in (0, 1) for key in ((-1 - s, 0), (1 + s, 1))]
    )
    middle = lay([(3, 0), (-3, 1), (-3, 0), (3, 1)])
    late = lay([(-4, 0), (4, 1)])
    pieces = (
        (early, join(act_half[1:], act_other[:2]), join(cot_half[1:], cot_other[:2])),
        (middle, join(act_half[:1], act_other[2:3]), join(cot_half[:1], cot_other[2:3])),
        (late, act_other[3], cot_other[3]),
    )
    down_total, gate_total, up_total = 0.0, 0.0, 0.0
    for whole, acts, cots in pieces:
        gate_total = gate_total + dot(acts, whole[1], FIRST)
        up_total = up_total + dot(acts, whole[2], FIRST)
        down_total = down_total + dot(whole[0], cots, FIRST)
    return (
        result[0],
        result[1],
        gate_total.astype(BF16),
        up_total.astype(BF16),
        down_total.astype(BF16),
    )


def solution(mesh):
    return jax.shard_map(
        local,
        mesh=mesh,
        in_specs=(
            P(("depth", "col"), "row"),
            P("row", "col"),
            P("row", "col"),
            P("col", "row"),
            P(("depth", "col"), "row"),
        ),
        out_specs=(
            P(("depth", "col"), "row"),
            P(("depth", "col"), "row"),
            P(("row", "depth"), "col"),
            P(("row", "depth"), "col"),
            P("col", ("row", "depth")),
        ),
        check_vma=False,
    )
```

```python
import jax
import jax.numpy as jnp
from jax import lax
from jax.sharding import PartitionSpec as P

AXES = ("row", "col", "depth")
LAST = (((1,), (1,)), ((), ()))
FIRST = (((0,), (0,)), ((), ()))
F32 = jnp.float32
BF16 = jnp.bfloat16


def send(value, dx=0, dy=0, dz=0, flip=0):
    pairs = []
    for i in range(256):
        row, col, depth = i // 32, i // 2 % 16, i % 2
        z = (depth * 4 + row // 2 + dz) % 8
        core = row % 2 ^ flip
        y, x = (col // 4 + dy) % 4, (col % 4 + dx) % 4
        pairs.append((i, ((z % 4 * 2 + core) * 16 + y * 4 + x) * 2 + z // 4))
    return lax.ppermute(value, AXES, pairs)


def step(value, axis, by):
    return send(value, **{axis: by})


def behind(value, *done):
    return lax.optimization_barrier((value, *done))[0]


def gather_ring(value, axis):
    half = value.shape[0] // 2
    before = step(value, axis, 1)
    after = step(value, axis, -1)
    low = step(before[:half], axis, 1)
    high = step(after[half:], axis, -1)
    return [value, after, jnp.concatenate([low, high]), before]


def gather_line(value, axis):
    far = step(value, axis, 2)
    return jnp.stack([value, step(value, axis, -1), far, step(value, axis, 1)])


def scatter_ring(blocks, axis, done):
    here, after, far, before = blocks
    half = here.shape[0] // 2
    up = step(far[:half].astype(BF16), axis, 1).astype(F32)
    down = step(far[half:].astype(BF16), axis, -1).astype(F32)
    after = jnp.concatenate([after[:half].astype(F32) + up, after[half:].astype(F32)]).astype(BF16)
    before = jnp.concatenate([before[:half].astype(F32), before[half:].astype(F32) + down]).astype(BF16)
    after, before = behind(after, *done), behind(before, *done)
    return here.astype(F32) + step(after, axis, 1).astype(F32) + step(before, axis, -1).astype(F32)


def scatter_line(blocks, axis):
    here, after, far, before = blocks
    total = here + step(after.astype(BF16), axis, 1).astype(F32)
    total = total + step(before.astype(BF16), axis, -1).astype(F32)
    return total + step(far.astype(BF16), axis, 2).astype(F32)


def scatter_plane(value, axes, done, done_late):
    place = 1 if axes[0] == "dy" else 2
    lines = scatter_ring([jnp.take(value, j, axis=place) for j in range(4)], axes[0], done)
    lines = behind(lines, *done_late)
    return scatter_line([lines[:, j] for j in range(4)], axes[1])


def dot(a, b, dims=(((1,), (0,)), ((), ()))):
    return lax.dot_general(a, b, dims, preferred_element_type=F32)


def half_of(value, which, axis):
    size = value.shape[axis] // 2
    return lax.dynamic_slice_in_dim(value, which * size, size, axis)


def pick(value, index, axis):
    return lax.dynamic_index_in_dim(value, index, axis, keepdims=False)


def local(activations, gate_weight, up_weight, down_weight, output_grad):
    tokens, feats = activations.shape
    units = gate_weight.shape[1]
    group = tokens // 8
    rows = 16 * group
    hu = units // 2
    row = lax.axis_index("row")
    line, core = row // 2, row % 2
    depth = lax.axis_index("depth")

    pair = jnp.stack([activations, output_grad]).reshape(2, 8, group, feats)
    foreign = send(lax.dynamic_slice_in_dim(pair[:, 1:7], line, 3, 1), dz=4)
    chosen = []
    for s in range(4):
        right = pick(pair, jnp.maximum(line - s, 0), 1)
        left = pick(pair, jnp.minimum(4 + line + s, 7), 1)
        if s > 0:
            right = jnp.where(line >= s, right, foreign[:, 3 - s])
            left = jnp.where(line + s <= 3, left, foreign[:, s - 1])
        chosen.append(jnp.stack([right, left], axis=1))
    chosen = jnp.stack(chosen, axis=1)
    lines = lax.optimization_barrier((gather_line(chosen[0], "dx"), gather_line(chosen[1], "dy")))
    act_ring = gather_ring(lines[0], "dy")
    act = jnp.stack(act_ring)
    cot = jnp.swapaxes(jnp.stack(gather_ring(lines[1], "dx")), 0, 1)
    act = jnp.transpose(act, (2, 3, 0, 1, 4, 5)).reshape(4, 2 * rows, feats)
    cot = jnp.transpose(cot, (2, 3, 0, 1, 4, 5)).reshape(4, 2 * rows, feats)

    gate_late, up_late, down_late = behind((gate_weight, up_weight, down_weight), act_ring[1])
    own_in = jnp.concatenate([half_of(gate_late, core, 1), half_of(up_late, core, 1)], axis=1)
    own_down = half_of(down_late, core, 0)
    sib_in = jnp.concatenate([half_of(gate_late, 1 - core, 1), half_of(up_late, 1 - core, 1)], axis=1)
    sib_in = send(sib_in, flip=1)
    sib_down = send(half_of(down_late, 1 - core, 0), flip=1)

    others = send(behind(half_of(chosen, 1 - depth, 4), lines), dz=4)
    act_sib = [send(act[0], flip=1), send(act[1:], flip=1)]
    cot_sib = [send(cot[0], flip=1), send(cot[1:], flip=1)]

    def partial(a, c, a2, c2):
        first = dot(a, own_in) + dot(a2, sib_in)
        second = dot(c, own_down, LAST) + dot(c2, sib_down, LAST)
        return jnp.concatenate([first, second], axis=1)

    sums = partial(act[0], cot[0], act_sib[0], cot_sib[0])
    message = sums.astype(BF16)
    act_rest, cot_rest = act[1:], cot[1:]
    for s in range(1, 4):
        right = send(message[:rows], dz=1)
        left = send(message[rows:], dz=-1)
        if s == 1:
            act_late, cot_late, others = behind((act_rest, cot_rest, others), right, left)
        else:
            act_rest, cot_rest = act_late, cot_late
        sums = partial(act_rest[s - 1], cot_rest[s - 1], act_sib[1][s - 1], cot_sib[1][s - 1])
        sums = sums + jnp.concatenate([right, left]).astype(F32)
        message = sums.astype(BF16)
    others = jnp.stack(gather_ring(gather_line(others, "dx"), "dy"))
    others = jnp.transpose(others, (2, 3, 4, 0, 1, 5, 6)).reshape(2, 4, 2 * rows, feats // 2)

    gate_sums, up_sums, hidden_grad = sums[:, :hu], sums[:, hu : 2 * hu], sums[:, 2 * hu :]
    sigmoid_gate = jax.nn.sigmoid(gate_sums)
    activated = gate_sums * sigmoid_gate
    hidden = (activated * up_sums).astype(BF16)
    gate_grad = (
        hidden_grad * up_sums * sigmoid_gate * (1.0 + gate_sums * (1.0 - sigmoid_gate))
    ).astype(BF16)
    up_grad = (hidden_grad * activated).astype(BF16)

    def sides(j, value):
        part[j, 0], part[j, 1] = value[:, :rows], value[:, rows:]

    def exchange(j, value):
        theirs = send(value, flip=1)
        sib_part[j, 0], sib_part[j, 1] = theirs[:, :rows], theirs[:, rows:]
        return theirs

    part, sib_part = {}, {}
    chunk = jnp.stack([hidden, gate_grad, up_grad])
    before, after = send(chunk, dz=1), send(chunk, dz=-1)
    exchange(0, chunk), exchange(-1, before), exchange(1, after)
    sides(0, chunk), sides(-1, before), sides(1, after)

    def onward(key_right, key_left, done):
        for (j, side), by in ((key_right, 1), (key_left, -1)):
            part[j, side] = send(behind(part[j + by, side], *done), dz=by)

    def onward_sib(*keys):
        for key in keys:
            sib_part[key] = send(part[key], flip=1)
        return [sib_part[key] for key in keys]

    onward((-2, 1), (2, 0), ())
    def lay(keys):
        mine = jnp.concatenate([part[key] for key in keys], axis=1)
        theirs = jnp.concatenate([sib_part[key] for key in keys], axis=1)
        return jnp.where(
            core == 0,
            jnp.concatenate([mine, theirs], axis=2),
            jnp.concatenate([theirs, mine], axis=2),
        )

    def outputs(keys):
        whole = lay(keys)
        shape = (len(keys), 4, 4, group, feats)
        layer = dot(whole[0], down_weight)
        inputs = dot(whole[1], gate_weight, LAST) + dot(whole[2], up_weight, LAST)
        return layer.astype(BF16).reshape(shape), inputs.astype(BF16).reshape(shape)

    first = outputs([(-1, 0), (0, 0), (1, 0), (-1, 1), (0, 1), (1, 1)])
    part[-2, 1], part[2, 0], first = lax.optimization_barrier((part[-2, 1], part[2, 0], first))
    second = onward_sib((-2, 1), (2, 0))
    onward((-2, 0), (2, 1), [part[-2, 1], part[2, 0]])
    third = onward_sib((-2, 0), (2, 1))
    whole_before = jnp.concatenate([part[-2, 0], part[-2, 1]], axis=1)
    whole_after = jnp.concatenate([part[2, 0], part[2, 1]], axis=1)
    before = send(behind(whole_before, *second), dz=1)
    after = send(behind(whole_after, *second), dz=-1)
    sides(-3, before), sides(3, after)
    exchange(-3, before), exchange(3, after)
    onward((-4, 0), (4, 1), third)
    last = onward_sib((-4, 0), (4, 1))

    more = outputs([(2, 0), (-2, 1)])
    layer, inputs = [jnp.concatenate([a[:3], b, a[3:]]) for a, b in zip(first, more)]
    done, done_late = (part[-2, 0], part[2, 1]), (part[-3, 0], part[3, 1])
    layer = scatter_plane(layer, ("dy", "dx"), done, done_late)
    inputs = scatter_plane(inputs, ("dx", "dy"), done, done_late)
    both = jnp.stack([layer, inputs]).astype(BF16)
    rights, lefts = both[:, :4], both[:, 4:]
    away = lax.dynamic_slice_in_dim(jnp.concatenate([lefts, rights], axis=1), 3 - line, 5, 1)
    away = behind(away, *last)
    back = send(away, dz=4)
    result = []
    for j in range(4):
        result.append(jnp.where(line <= j, back[:, j + 1], pick(rights, jnp.minimum(j - line + 4, 3), 1)))
    for j in range(4):
        result.append(jnp.where(line >= j, back[:, j], pick(lefts, jnp.maximum(j - line - 1, 0), 1)))
    result = jnp.stack(result, axis=1).reshape(2, tokens, feats)

    act_half, cot_half = half_of(act, depth, 2), half_of(cot, depth, 2)
    act_other, cot_other = others[0], others[1]
    hf = feats // 2

    def join(mine, theirs):
        return jnp.concatenate([mine.reshape(-1, hf), theirs.reshape(-1, hf)])

    early = lay(
        [key for s in (1, 2, 3) for key in ((3 - s, 0), (s - 3, 1))]
        + [key for s in (0, 1) for key in ((-1 - s, 0), (1 + s, 1))]
    )
    middle = behind(lay([(3, 0), (-3, 1), (-3, 0), (3, 1)]), away)
    late = behind(lay([(-4, 0), (4, 1)]), away)
    pieces = (
        (early, join(act_half[1:], act_other[:2]), join(cot_half[1:], cot_other[:2])),
        (middle, join(act_half[:1], act_other[2:3]), join(cot_half[:1], cot_other[2:3])),
        (late, act_other[3], cot_other[3]),
    )
    down_total, gate_total, up_total = 0.0, 0.0, 0.0
    for whole, acts, cots in pieces:
        gate_total = gate_total + dot(acts, whole[1], FIRST)
        up_total = up_total + dot(acts, whole[2], FIRST)
        down_total = down_total + dot(whole[0], cots, FIRST)
    return (
        result[0],
        result[1],
        gate_total.astype(BF16),
        up_total.astype(BF16),
        down_total.astype(BF16),
    )


def solution(mesh):
    return jax.shard_map(
        local,
        mesh=mesh,
        in_specs=(
            P(("depth", "col"), "row"),
            P("row", "col"),
            P("row", "col"),
            P("col", "row"),
            P(("depth", "col"), "row"),
        ),
        out_specs=(
            P(("depth", "col"), "row"),
            P(("depth", "col"), "row"),
            P(("row", "depth"), "col"),
            P(("row", "depth"), "col"),
            P("col", ("row", "depth")),
        ),
        check_vma=False,
    )
```

```python
import jax
import jax.numpy as jnp
from jax import lax
from jax.sharding import PartitionSpec as P

AXES = ("row", "col", "depth")
LAST = (((1,), (1,)), ((), ()))
FIRST = (((0,), (0,)), ((), ()))
F32 = jnp.float32
BF16 = jnp.bfloat16


def send(value, dx=0, dy=0, dz=0, flip=0):
    pairs = []
    for i in range(256):
        row, col, depth = i // 32, i // 2 % 16, i % 2
        z = (depth * 4 + row // 2 + dz) % 8
        core = row % 2 ^ flip
        y, x = (col // 4 + dy) % 4, (col % 4 + dx) % 4
        pairs.append((i, ((z % 4 * 2 + core) * 16 + y * 4 + x) * 2 + z // 4))
    return lax.ppermute(value, AXES, pairs)


def step(value, axis, by):
    return send(value, **{axis: by})


def behind(value, *done):
    return lax.optimization_barrier((value, *done))[0]


def gather_ring(value, axis):
    half = value.shape[0] // 2
    before = step(value, axis, 1)
    after = step(value, axis, -1)
    low = step(before[:half], axis, 1)
    high = step(after[half:], axis, -1)
    return [value, after, jnp.concatenate([low, high]), before]


def gather_line(value, axis):
    far = step(value, axis, 2)
    return jnp.stack([value, step(value, axis, -1), far, step(value, axis, 1)])


def scatter_first(value, axis):
    blocks = [jnp.take(value, j, axis=1 if axis == "dy" else 2) for j in range(4)]
    half = value.shape[0] // 2
    return blocks, (step(blocks[2][:half], axis, 1), step(blocks[2][half:], axis, -1))


def scatter_second(blocks, halves, axis):
    here, after, far, before = [block.astype(F32) for block in blocks]
    up, down = [half.astype(F32) for half in halves]
    half = here.shape[0] // 2
    after = jnp.concatenate([after[:half] + up, after[half:]]).astype(BF16)
    before = jnp.concatenate([before[:half], before[half:] + down]).astype(BF16)
    return here + step(after, axis, 1).astype(F32) + step(before, axis, -1).astype(F32)


def scatter_line(lines, axis):
    col = lax.axis_index("col")
    if axis == "dx":
        me, groups = col % 4, [[y * 4 + x for x in range(4)] for y in range(4)]
    else:
        me, groups = col // 4, [[y * 4 + x for y in range(4)] for x in range(4)]
    lines = lines.astype(BF16)
    lines = lax.dynamic_slice_in_dim(jnp.concatenate([lines, lines], axis=1), (4 - me) % 4, 4, 1)
    lines = lax.all_to_all(lines, "col", 1, 1, axis_index_groups=groups, tiled=True)
    return jnp.sum(lines.astype(F32), axis=1)


def dot(a, b, dims=(((1,), (0,)), ((), ()))):
    return lax.dot_general(a, b, dims, preferred_element_type=F32)


def half_of(value, which, axis):
    size = value.shape[axis] // 2
    return lax.dynamic_slice_in_dim(value, which * size, size, axis)


def pick(value, index, axis):
    return lax.dynamic_index_in_dim(value, index, axis, keepdims=False)


def local(activations, gate_weight, up_weight, down_weight, output_grad):
    tokens, feats = activations.shape
    units = gate_weight.shape[1]
    group = tokens // 8
    rows = 16 * group
    hu = units // 2
    row = lax.axis_index("row")
    line, core = row // 2, row % 2
    depth = lax.axis_index("depth")

    pair = jnp.stack([activations, output_grad]).reshape(2, 8, group, feats)
    foreign = send(lax.dynamic_slice_in_dim(pair[:, 1:7], line, 3, 1), dz=4)
    chosen = []
    for s in range(4):
        right = pick(pair, jnp.maximum(line - s, 0), 1)
        left = pick(pair, jnp.minimum(4 + line + s, 7), 1)
        if s > 0:
            right = jnp.where(line >= s, right, foreign[:, 3 - s])
            left = jnp.where(line + s <= 3, left, foreign[:, s - 1])
        chosen.append(jnp.stack([right, left], axis=1))
    chosen = jnp.stack(chosen, axis=1)
    lines = lax.optimization_barrier((gather_line(chosen[0], "dx"), gather_line(chosen[1], "dy")))
    act_ring = gather_ring(lines[0], "dy")
    act = jnp.stack(act_ring)
    cot = jnp.swapaxes(jnp.stack(gather_ring(lines[1], "dx")), 0, 1)
    act = jnp.transpose(act, (2, 3, 0, 1, 4, 5)).reshape(4, 2 * rows, feats)
    cot = jnp.transpose(cot, (2, 3, 0, 1, 4, 5)).reshape(4, 2 * rows, feats)

    gate_late, up_late, down_late = behind((gate_weight, up_weight, down_weight), act_ring[1])
    own_in = jnp.concatenate([half_of(gate_late, core, 1), half_of(up_late, core, 1)], axis=1)
    own_down = half_of(down_late, core, 0)
    other_in = jnp.concatenate([half_of(gate_late, 1 - core, 1), half_of(up_late, 1 - core, 1)], axis=1)
    other_down = half_of(down_late, 1 - core, 0)
    sib_in, sib_down = send(other_in, flip=1), send(other_down, flip=1)

    others = send(behind(half_of(chosen, 1 - depth, 4), lines), dz=4)
    act_sib = [send(act[0], flip=1), send(act[1:], flip=1)]
    cot_sib = [send(cot[0], flip=1), send(cot[1:], flip=1)]

    def partial(a, c, a2, c2):
        first = dot(a, own_in) + dot(a2, sib_in)
        second = dot(c, own_down, LAST) + dot(c2, sib_down, LAST)
        return jnp.concatenate([first, second], axis=1)

    sums = partial(act[0], cot[0], act_sib[0], cot_sib[0])
    message = sums.astype(BF16)
    act_rest, cot_rest = act[1:], cot[1:]
    for s in range(1, 4):
        right = send(message[:rows], dz=1)
        left = send(message[rows:], dz=-1)
        if s == 1:
            act_late, cot_late = behind((act_rest, cot_rest), right, left)
        else:
            act_rest, cot_rest = act_late, cot_late
        sums = partial(act_rest[s - 1], cot_rest[s - 1], act_sib[1][s - 1], cot_sib[1][s - 1])
        if s == 2:
            sums, others = lax.optimization_barrier((sums, others))
        sums = sums + jnp.concatenate([right, left]).astype(F32)
        message = sums.astype(BF16)

    gate_sums, up_sums, hidden_grad = sums[:, :hu], sums[:, hu : 2 * hu], sums[:, 2 * hu :]
    sigmoid_gate = jax.nn.sigmoid(gate_sums)
    activated = gate_sums * sigmoid_gate
    hidden = (activated * up_sums).astype(BF16)
    gate_grad = (
        hidden_grad * up_sums * sigmoid_gate * (1.0 + gate_sums * (1.0 - sigmoid_gate))
    ).astype(BF16)
    up_grad = (hidden_grad * activated).astype(BF16)

    def outputs_of(mine, theirs):
        mine, theirs = jnp.concatenate(mine), jnp.concatenate(theirs)
        layer = dot(mine[:, :hu], own_down) + dot(theirs[:, :hu], other_down)
        inputs = dot(mine[:, hu:], own_in, LAST) + dot(theirs[:, hu:], other_in, LAST)
        return layer.astype(BF16), inputs.astype(BF16)

    chunk = {0: jnp.concatenate([hidden, gate_grad, up_grad], axis=1)}
    sibling = {}
    for j in range(1, 3):
        chunk[-j] = send(chunk[1 - j], dz=1)
        chunk[j] = send(chunk[j - 1], dz=-1)
        if j == 1:
            sibling[0] = send(chunk[0], flip=1)
        if j == 2:
            chunk[-2], chunk[2], near = lax.optimization_barrier((chunk[-2], chunk[2], near))
        sibling[-j], sibling[j] = send(chunk[-j], flip=1), send(chunk[j], flip=1)
        if j == 1:
            near = outputs_of((chunk[-1], chunk[0], chunk[1]), (sibling[-1], sibling[0], sibling[1]))
        if j == 2:
            more = outputs_of((chunk[2][:rows], chunk[-2][rows:]), (sibling[2][:rows], sibling[-2][rows:]))

    shape = (8, 4, 4, group, feats)
    layer, inputs = [jnp.concatenate(pair).reshape(shape) for pair in zip(near, more)]
    layer, layer_halves = scatter_first(layer, "dy")
    inputs, inputs_halves = scatter_first(inputs, "dx")
    chunk[-3] = send(behind(chunk[-2], *layer_halves), dz=1)
    chunk[3] = send(behind(chunk[2], *layer_halves), dz=-1)
    sibling[-3], sibling[3] = send(chunk[-3], flip=1), send(chunk[3], flip=1)
    far_right, far_left = send(chunk[-3][:rows], dz=1), send(chunk[3][rows:], dz=-1)
    last = [send(far_right, flip=1), send(far_left, flip=1)]
    chunk[4], sibling[4] = jnp.concatenate([far_right, far_left]), jnp.concatenate(last)
    layer = scatter_line(scatter_second(layer, layer_halves, "dy"), "dx")
    inputs = scatter_line(scatter_second(inputs, inputs_halves, "dx"), "dy")
    both = jnp.stack([layer, inputs]).astype(BF16)

    others = gather_line(others, "dx")
    others = jnp.stack(gather_ring(others, "dy"))
    others = jnp.transpose(others, (2, 3, 4, 0, 1, 5, 6)).reshape(2, 4, 2, rows, feats // 2)

    rights = jnp.stack([both[:, i] for i in (0, 2, 4, 6)], axis=1)
    lefts = jnp.stack([both[:, i] for i in (7, 1, 3, 5)], axis=1)
    hf = feats // 2
    act_half = half_of(act, depth, 2).reshape(4, 2, rows, hf)
    cot_half = half_of(cot, depth, 2).reshape(4, 2, rows, hf)

    def matching(chosen, other, keys):
        parts = []
        for j in keys:
            parts.append(chosen[3 - j, 0] if j in (0, 1, 2, 3) else other[(-1 - j) % 8, 0])
            parts.append(chosen[j + 3, 1] if j in (0, -1, -2, -3) else other[j - 1, 1])
        return jnp.concatenate(parts)

    away = lax.dynamic_slice_in_dim(jnp.concatenate([lefts, rights], axis=1), 3 - line, 5, 1)
    mine_in, theirs_in, mine_down, theirs_down = 0.0, 0.0, 0.0, 0.0
    for keys in ((2, 1, 0, -1, -2), (3, -3), (4,)):
        mine = jnp.concatenate([chunk[j] for j in keys])
        theirs = jnp.concatenate([sibling[j] for j in keys])
        late = (away,) if keys[0] > 2 else (*layer_halves, *inputs_halves)
        mine, theirs = behind((mine, theirs), *late)
        acts = matching(act_half, others[0], keys)
        cots = matching(cot_half, others[1], keys)
        mine_in = mine_in + dot(acts, mine[:, hu:], FIRST)
        theirs_in = theirs_in + dot(acts, theirs[:, hu:], FIRST)
        mine_down = mine_down + dot(mine[:, :hu], cots, FIRST)
        theirs_down = theirs_down + dot(theirs[:, :hu], cots, FIRST)
        if keys[0] == 2:
            away, mine_in, theirs_in, mine_down, theirs_down = lax.optimization_barrier(
                (away, mine_in, theirs_in, mine_down, theirs_down)
            )

    back = send(away, dz=4)
    result = []
    for j in range(4):
        result.append(jnp.where(line <= j, back[:, j + 1], pick(rights, jnp.minimum(j - line + 4, 3), 1)))
    for j in range(4):
        result.append(jnp.where(line >= j, back[:, j], pick(lefts, jnp.maximum(j - line - 1, 0), 1)))
    result = jnp.stack(result, axis=1).reshape(2, tokens, feats)

    def ordered(mine, theirs, axis):
        mine, theirs = mine.astype(BF16), theirs.astype(BF16)
        first, second = jnp.where(core == 0, mine, theirs), jnp.where(core == 0, theirs, mine)
        return jnp.concatenate([first, second], axis=axis)

    return (
        result[0],
        result[1],
        ordered(mine_in[:, :hu], theirs_in[:, :hu], 1),
        ordered(mine_in[:, hu:], theirs_in[:, hu:], 1),
        ordered(mine_down, theirs_down, 0),
    )


def solution(mesh):
    return jax.shard_map(
        local,
        mesh=mesh,
        in_specs=(
            P(("depth", "col"), "row"),
            P("row", "col"),
            P("row", "col"),
            P("col", "row"),
            P(("depth", "col"), "row"),
        ),
        out_specs=(
            P(("depth", "col"), "row"),
            P(("depth", "col"), "row"),
            P(("row", "depth"), "col"),
            P(("row", "depth"), "col"),
            P("col", ("row", "depth")),
        ),
        check_vma=False,
    )
```

```python
import jax
import jax.numpy as jnp
from jax import lax
from jax.sharding import PartitionSpec as P

AXES = ("row", "col", "depth")
LAST = (((1,), (1,)), ((), ()))
FIRST = (((0,), (0,)), ((), ()))
F32 = jnp.float32
BF16 = jnp.bfloat16


def send(value, dx=0, dy=0, dz=0, flip=0):
    pairs = []
    for i in range(256):
        row, col, depth = i // 32, i // 2 % 16, i % 2
        z = (depth * 4 + row // 2 + dz) % 8
        core = row % 2 ^ flip
        y, x = (col // 4 + dy) % 4, (col % 4 + dx) % 4
        pairs.append((i, ((z % 4 * 2 + core) * 16 + y * 4 + x) * 2 + z // 4))
    return lax.ppermute(value, AXES, pairs)


def step(value, axis, by):
    return send(value, **{axis: by})


def behind(value, *done):
    return lax.optimization_barrier((value, *done))[0]


def gather_ring(value, axis):
    half = value.shape[0] // 2
    before = step(value, axis, 1)
    after = step(value, axis, -1)
    low = step(before[:half], axis, 1)
    high = step(after[half:], axis, -1)
    return [value, after, jnp.concatenate([low, high]), before]


def gather_line(value, axis):
    far = step(value, axis, 2)
    return jnp.stack([value, step(value, axis, -1), far, step(value, axis, 1)])


def scatter_first(value, axis):
    blocks = [jnp.take(value, j, axis=1 if axis == "dy" else 2) for j in range(4)]
    half = value.shape[0] // 2
    return blocks, (step(blocks[2][:half], axis, 1), step(blocks[2][half:], axis, -1))


def scatter_second(blocks, halves, axis):
    here, after, far, before = [block.astype(F32) for block in blocks]
    up, down = [half.astype(F32) for half in halves]
    half = here.shape[0] // 2
    after = jnp.concatenate([after[:half] + up, after[half:]]).astype(BF16)
    before = jnp.concatenate([before[:half], before[half:] + down]).astype(BF16)
    return here + step(after, axis, 1).astype(F32) + step(before, axis, -1).astype(F32)


def scatter_line(lines, axis):
    here, after, far, before = [lines[:, j] for j in range(4)]
    total = here + step(after.astype(BF16), axis, 1).astype(F32)
    total = total + step(before.astype(BF16), axis, -1).astype(F32)
    return total + step(far.astype(BF16), axis, 2).astype(F32)


def absolute(value, axis):
    col = lax.axis_index("col")
    me = col % 4 if axis == "dx" else col // 4
    return lax.dynamic_slice_in_dim(jnp.concatenate([value, value], axis=1), (4 - me) % 4, 4, 1)


def exchange(value, axis):
    if axis == "dx":
        groups = [[y * 4 + x for x in range(4)] for y in range(4)]
    else:
        groups = [[y * 4 + x for y in range(4)] for x in range(4)]
    value = lax.all_to_all(value, "col", 1, 1, axis_index_groups=groups, tiled=True)
    return jnp.sum(value.astype(F32), axis=1)


def dot(a, b, dims=(((1,), (0,)), ((), ()))):
    return lax.dot_general(a, b, dims, preferred_element_type=F32)


def half_of(value, which, axis):
    size = value.shape[axis] // 2
    return lax.dynamic_slice_in_dim(value, which * size, size, axis)


def pick(value, index, axis):
    return lax.dynamic_index_in_dim(value, index, axis, keepdims=False)


def local(activations, gate_weight, up_weight, down_weight, output_grad):
    tokens, feats = activations.shape
    units = gate_weight.shape[1]
    group = tokens // 8
    rows = 16 * group
    hu = units // 2
    row = lax.axis_index("row")
    line, core = row // 2, row % 2
    depth = lax.axis_index("depth")

    pair = jnp.stack([activations, output_grad]).reshape(2, 8, group, feats)
    foreign = send(lax.dynamic_slice_in_dim(pair[:, 1:7], line, 3, 1), dz=4)
    chosen = []
    for s in range(4):
        right = pick(pair, jnp.maximum(line - s, 0), 1)
        left = pick(pair, jnp.minimum(4 + line + s, 7), 1)
        if s > 0:
            right = jnp.where(line >= s, right, foreign[:, 3 - s])
            left = jnp.where(line + s <= 3, left, foreign[:, s - 1])
        chosen.append(jnp.stack([right, left], axis=1))
    chosen = jnp.stack(chosen, axis=1)
    lines = lax.optimization_barrier((gather_line(chosen[0], "dx"), gather_line(chosen[1], "dy")))
    act_ring = gather_ring(lines[0], "dy")
    act = jnp.stack(act_ring)
    cot = jnp.swapaxes(jnp.stack(gather_ring(lines[1], "dx")), 0, 1)
    act = jnp.transpose(act, (2, 3, 0, 1, 4, 5)).reshape(4, 2 * rows, feats)
    cot = jnp.transpose(cot, (2, 3, 0, 1, 4, 5)).reshape(4, 2 * rows, feats)

    gate_late, up_late, down_late = behind((gate_weight, up_weight, down_weight), act_ring[1])
    own_in = jnp.concatenate([half_of(gate_late, core, 1), half_of(up_late, core, 1)], axis=1)
    own_down = half_of(down_late, core, 0)
    sib_in = jnp.concatenate([half_of(gate_late, 1 - core, 1), half_of(up_late, 1 - core, 1)], axis=1)
    sib_in, sib_down = send(sib_in, flip=1), send(half_of(down_late, 1 - core, 0), flip=1)

    others = send(behind(half_of(chosen, 1 - depth, 4), lines), dz=4)
    act_sib = [send(act[0], flip=1), send(act[1:], flip=1)]
    cot_sib = [send(cot[0], flip=1), send(cot[1:], flip=1)]

    def partial(a, c, a2, c2):
        first = dot(a, own_in) + dot(a2, sib_in)
        second = dot(c, own_down, LAST) + dot(c2, sib_down, LAST)
        return jnp.concatenate([first, second], axis=1)

    sums = partial(act[0], cot[0], act_sib[0], cot_sib[0])
    message = sums.astype(BF16)
    act_rest, cot_rest = act[1:], cot[1:]
    for s in range(1, 4):
        right = send(message[:rows], dz=1)
        left = send(message[rows:], dz=-1)
        if s == 1:
            act_late, cot_late = behind((act_rest, cot_rest), right, left)
        else:
            act_rest, cot_rest = act_late, cot_late
        sums = partial(act_rest[s - 1], cot_rest[s - 1], act_sib[1][s - 1], cot_sib[1][s - 1])
        if s == 2:
            sums, others = lax.optimization_barrier((sums, others))
            others = gather_line(others, "dx")
        sums = sums + jnp.concatenate([right, left]).astype(F32)
        message = sums.astype(BF16)

    gate_sums, up_sums, hidden_grad = sums[:, :hu], sums[:, hu : 2 * hu], sums[:, 2 * hu :]
    sigmoid_gate = jax.nn.sigmoid(gate_sums)
    activated = gate_sums * sigmoid_gate
    hidden = (activated * up_sums).astype(BF16)
    gate_grad = (
        hidden_grad * up_sums * sigmoid_gate * (1.0 + gate_sums * (1.0 - sigmoid_gate))
    ).astype(BF16)
    up_grad = (hidden_grad * activated).astype(BF16)

    def lay(mine, theirs):
        mine, theirs = jnp.concatenate(mine, axis=1), jnp.concatenate(theirs, axis=1)
        return jnp.where(
            core == 0,
            jnp.concatenate([mine, theirs], axis=2),
            jnp.concatenate([theirs, mine], axis=2),
        )

    def outputs_of(mine, theirs):
        whole = lay(mine, theirs)
        layer = dot(whole[0], down_weight)
        inputs = dot(whole[1], gate_weight, LAST) + dot(whole[2], up_weight, LAST)
        shape = (-1, 4, 4, group, feats)
        return absolute(layer.astype(BF16).reshape(shape), "dy"), inputs.astype(BF16).reshape(shape)

    chunk = {0: jnp.stack([hidden, gate_grad, up_grad])}
    sibling = {}
    for j in range(1, 3):
        chunk[-j] = send(chunk[1 - j], dz=1)
        chunk[j] = send(chunk[j - 1], dz=-1)
        if j == 1:
            sibling[0] = send(chunk[0], flip=1)
        if j == 2:
            chunk[-2], chunk[2], near = lax.optimization_barrier((chunk[-2], chunk[2], near))
        sibling[-j], sibling[j] = send(chunk[-j], flip=1), send(chunk[j], flip=1)
        if j == 1:
            near = outputs_of([chunk[i] for i in (-1, 0, 1)], [sibling[i] for i in (-1, 0, 1)])
        if j == 2:
            more = outputs_of(
                (chunk[2][:, :rows], chunk[-2][:, rows:]), (sibling[2][:, :rows], sibling[-2][:, rows:])
            )

    others = jnp.stack(gather_ring(behind(others, sibling[0]), "dy"))
    others = jnp.transpose(others, (2, 3, 4, 0, 1, 5, 6)).reshape(2, 4, 2, rows, feats // 2)

    layer, inputs = [jnp.concatenate(pair) for pair in zip(near, more)]
    inputs, halves = scatter_first(inputs, "dx")
    chunk[-3], chunk[3] = send(chunk[-2], dz=1), send(chunk[2], dz=-1)
    sibling[-3], sibling[3] = send(chunk[-3], flip=1), send(chunk[3], flip=1)
    far_right, far_left = send(chunk[-3][:, :rows], dz=1), send(chunk[3][:, rows:], dz=-1)
    last = [send(far_right, flip=1), send(far_left, flip=1)]
    layer = exchange(layer, "dy")
    layer = exchange(absolute(layer.astype(BF16), "dx"), "dx")
    inputs = scatter_line(scatter_second(inputs, halves, "dx"), "dy")
    both = jnp.stack([layer, inputs]).astype(BF16)
    rights = jnp.stack([both[:, i] for i in (0, 2, 4, 6)], axis=1)
    lefts = jnp.stack([both[:, i] for i in (7, 1, 3, 5)], axis=1)
    away = lax.dynamic_slice_in_dim(jnp.concatenate([lefts, rights], axis=1), 3 - line, 5, 1)
    back = behind(send(away, dz=4), *last)
    result = []
    for j in range(4):
        result.append(jnp.where(line <= j, back[:, j + 1], pick(rights, jnp.minimum(j - line + 4, 3), 1)))
    for j in range(4):
        result.append(jnp.where(line >= j, back[:, j], pick(lefts, jnp.maximum(j - line - 1, 0), 1)))
    result = jnp.stack(result, axis=1).reshape(2, tokens, feats)

    hf = feats // 2
    act_half = half_of(act, depth, 2).reshape(4, 2, rows, hf)
    cot_half = half_of(cot, depth, 2).reshape(4, 2, rows, hf)

    def matching(chosen, other, keys):
        parts = []
        for j in keys:
            parts.append(chosen[3 - j, 0] if j in (0, 1, 2, 3) else other[(-1 - j) % 8, 0])
            parts.append(chosen[j + 3, 1] if j in (0, -1, -2, -3) else other[j - 1, 1])
        return jnp.concatenate(parts)

    def gradients(keys, mine, theirs):
        whole = lay(mine, theirs)
        acts, cots = matching(act_half, others[0], keys), matching(cot_half, others[1], keys)
        return dot(acts, whole[1], FIRST), dot(acts, whole[2], FIRST), dot(whole[0], cots, FIRST)

    keys = (2, 1, 0, -1, -2)
    mine, theirs = behind(([chunk[j] for j in keys], [sibling[j] for j in keys]), *halves)
    early = lax.optimization_barrier(gradients(keys, mine, theirs))
    pieces = behind(((chunk[3], chunk[-3]), (sibling[3], sibling[-3]), (far_right, far_left), last), away)
    middle, late = gradients((3, -3), *pieces[:2]), gradients((4,), *pieces[2:])
    totals = [(a + b + c).astype(BF16) for a, b, c in zip(early, middle, late)]
    return result[0], result[1], *totals


def solution(mesh):
    return jax.shard_map(
        local,
        mesh=mesh,
        in_specs=(
            P(("depth", "col"), "row"),
            P("row", "col"),
            P("row", "col"),
            P("col", "row"),
            P(("depth", "col"), "row"),
        ),
        out_specs=(
            P(("depth", "col"), "row"),
            P(("depth", "col"), "row"),
            P(("row", "depth"), "col"),
            P(("row", "depth"), "col"),
            P("col", ("row", "depth")),
        ),
        check_vma=False,
    )
```

```python
import jax
import jax.numpy as jnp
from jax import lax
from jax.sharding import PartitionSpec as P

AXES = ("row", "col", "depth")
LAST = (((1,), (1,)), ((), ()))
FIRST = (((0,), (0,)), ((), ()))
F32 = jnp.float32
BF16 = jnp.bfloat16


def send(value, dx=0, dy=0, dz=0, flip=0):
    pairs = []
    for i in range(256):
        row, col, depth = i // 32, i // 2 % 16, i % 2
        z = (depth * 4 + row // 2 + dz) % 8
        core = row % 2 ^ flip
        y, x = (col // 4 + dy) % 4, (col % 4 + dx) % 4
        pairs.append((i, ((z % 4 * 2 + core) * 16 + y * 4 + x) * 2 + z // 4))
    return lax.ppermute(value, AXES, pairs)


def step(value, axis, by):
    return send(value, **{axis: by})


def behind(value, *done):
    return lax.optimization_barrier((value, *done))[0]


def gather_ring(value, axis):
    half = value.shape[0] // 2
    before = step(value, axis, 1)
    after = step(value, axis, -1)
    low = step(before[:half], axis, 1)
    high = step(after[half:], axis, -1)
    return [value, after, jnp.concatenate([low, high]), before]


def gather_line(value, axis):
    far = step(value, axis, 2)
    return jnp.stack([value, step(value, axis, -1), far, step(value, axis, 1)])


def scatter_first(value, axis):
    blocks = [jnp.take(value, j, axis=1 if axis == "dy" else 2) for j in range(4)]
    half = value.shape[0] // 2
    return blocks, (step(blocks[2][:half], axis, 1), step(blocks[2][half:], axis, -1))


def scatter_second(blocks, halves, axis):
    here, after, far, before = [block.astype(F32) for block in blocks]
    up, down = [half.astype(F32) for half in halves]
    half = here.shape[0] // 2
    after = jnp.concatenate([after[:half] + up, after[half:]]).astype(BF16)
    before = jnp.concatenate([before[:half], before[half:] + down]).astype(BF16)
    after, before = step(after, axis, 1), step(before, axis, -1)
    return here + after.astype(F32) + before.astype(F32), (after, before)


def scatter_line(lines, axis):
    here, after, far, before = [lines[:, j] for j in range(4)]
    total = here + step(after.astype(BF16), axis, 1).astype(F32)
    total = total + step(before.astype(BF16), axis, -1).astype(F32)
    return total + step(far.astype(BF16), axis, 2).astype(F32)


def dot(a, b, dims=(((1,), (0,)), ((), ()))):
    return lax.dot_general(a, b, dims, preferred_element_type=F32)


def half_of(value, which, axis):
    size = value.shape[axis] // 2
    return lax.dynamic_slice_in_dim(value, which * size, size, axis)


def pick(value, index, axis):
    return lax.dynamic_index_in_dim(value, index, axis, keepdims=False)


def local(activations, gate_weight, up_weight, down_weight, output_grad):
    tokens, feats = activations.shape
    units = gate_weight.shape[1]
    group = tokens // 8
    rows = 16 * group
    hu = units // 2
    row = lax.axis_index("row")
    line, core = row // 2, row % 2
    depth = lax.axis_index("depth")

    pair = jnp.stack([activations, output_grad]).reshape(2, 8, group, feats)
    foreign = send(lax.dynamic_slice_in_dim(pair[:, 1:7], line, 3, 1), dz=4)
    chosen = []
    for s in range(4):
        right = pick(pair, jnp.maximum(line - s, 0), 1)
        left = pick(pair, jnp.minimum(4 + line + s, 7), 1)
        if s > 0:
            right = jnp.where(line >= s, right, foreign[:, 3 - s])
            left = jnp.where(line + s <= 3, left, foreign[:, s - 1])
        chosen.append(jnp.stack([right, left], axis=1))
    chosen = jnp.stack(chosen, axis=1)
    lines = lax.optimization_barrier((gather_line(chosen[0], "dx"), gather_line(chosen[1], "dy")))
    act_ring = gather_ring(lines[0], "dy")
    act = jnp.stack(act_ring)
    cot = jnp.swapaxes(jnp.stack(gather_ring(lines[1], "dx")), 0, 1)
    act = jnp.transpose(act, (2, 3, 0, 1, 4, 5)).reshape(4, 2 * rows, feats)
    cot = jnp.transpose(cot, (2, 3, 0, 1, 4, 5)).reshape(4, 2 * rows, feats)

    gate_late, up_late, down_late = behind((gate_weight, up_weight, down_weight), act_ring[1])
    own_in = jnp.concatenate([half_of(gate_late, core, 1), half_of(up_late, core, 1)], axis=1)
    own_down = half_of(down_late, core, 0)
    sib_in = jnp.concatenate([half_of(gate_late, 1 - core, 1), half_of(up_late, 1 - core, 1)], axis=1)
    sib_in, sib_down = send(sib_in, flip=1), send(half_of(down_late, 1 - core, 0), flip=1)

    others = send(behind(half_of(chosen, 1 - depth, 4), lines), dz=4)
    act_sib = [send(act[0], flip=1), send(act[1:], flip=1)]
    cot_sib = [send(cot[0], flip=1), send(cot[1:], flip=1)]

    def partial(a, c, a2, c2):
        first = dot(a, own_in) + dot(a2, sib_in)
        second = dot(c, own_down, LAST) + dot(c2, sib_down, LAST)
        return jnp.concatenate([first, second], axis=1)

    sums = partial(act[0], cot[0], act_sib[0], cot_sib[0])
    message = sums.astype(BF16)
    act_rest, cot_rest = act[1:], cot[1:]
    for s in range(1, 4):
        right = send(message[:rows], dz=1)
        left = send(message[rows:], dz=-1)
        if s == 1:
            act_late, cot_late = behind((act_rest, cot_rest), right, left)
        else:
            act_rest, cot_rest = act_late, cot_late
        sums = partial(act_rest[s - 1], cot_rest[s - 1], act_sib[1][s - 1], cot_sib[1][s - 1])
        if s == 2:
            sums, others = lax.optimization_barrier((sums, others))
            others = gather_line(others, "dx")
        sums = sums + jnp.concatenate([right, left]).astype(F32)
        message = sums.astype(BF16)

    gate_sums, up_sums, hidden_grad = sums[:, :hu], sums[:, hu : 2 * hu], sums[:, 2 * hu :]
    sigmoid_gate = jax.nn.sigmoid(gate_sums)
    activated = gate_sums * sigmoid_gate
    hidden = (activated * up_sums).astype(BF16)
    gate_grad = (
        hidden_grad * up_sums * sigmoid_gate * (1.0 + gate_sums * (1.0 - sigmoid_gate))
    ).astype(BF16)
    up_grad = (hidden_grad * activated).astype(BF16)

    def lay(mine, theirs):
        mine, theirs = jnp.concatenate(mine, axis=1), jnp.concatenate(theirs, axis=1)
        return jnp.where(
            core == 0,
            jnp.concatenate([mine, theirs], axis=2),
            jnp.concatenate([theirs, mine], axis=2),
        )

    def outputs_of(whole):
        layer = dot(whole[0], down_weight)
        inputs = dot(whole[1], gate_weight, LAST) + dot(whole[2], up_weight, LAST)
        shape = (-1, 4, 4, group, feats)
        return layer.astype(BF16).reshape(shape), inputs.astype(BF16).reshape(shape)

    others = jnp.stack(gather_ring(others, "dy"))
    others = jnp.transpose(others, (2, 3, 4, 0, 1, 5, 6)).reshape(2, 4, 2, rows, feats // 2)

    hf = feats // 2
    act_half = half_of(act, depth, 2).reshape(4, 2, rows, hf)
    cot_half = half_of(cot, depth, 2).reshape(4, 2, rows, hf)

    def matching(chosen, other, keys):
        parts = []
        for j in keys:
            parts.append(chosen[3 - j, 0] if j in (0, 1, 2, 3) else other[(-1 - j) % 8, 0])
            parts.append(chosen[j + 3, 1] if j in (0, -1, -2, -3) else other[j - 1, 1])
        return jnp.concatenate(parts)

    def gradients(keys, whole):
        acts, cots = matching(act_half, others[0], keys), matching(cot_half, others[1], keys)
        return dot(acts, whole[1], FIRST), dot(acts, whole[2], FIRST), dot(whole[0], cots, FIRST)

    chunk = {0: jnp.stack([hidden, gate_grad, up_grad])}
    sibling = {}
    for j in range(1, 3):
        chunk[-j] = send(chunk[1 - j], dz=1)
        chunk[j] = send(chunk[j - 1], dz=-1)
        if j == 1:
            sibling[0] = send(chunk[0], flip=1)
        if j == 2:
            chunk[-2], chunk[2], near, early = lax.optimization_barrier((chunk[-2], chunk[2], near, early))
        sibling[-j], sibling[j] = send(chunk[-j], flip=1), send(chunk[j], flip=1)
        if j == 1:
            whole = lay([chunk[i] for i in (-1, 0, 1)], [sibling[i] for i in (-1, 0, 1)])
            near, early = outputs_of(whole), gradients((-1, 0, 1), whole)
        if j == 2:
            whole = lay((chunk[2][:, :rows], chunk[-2][:, rows:]), (sibling[2][:, :rows], sibling[-2][:, rows:]))
            more = outputs_of(whole)

    layer, inputs = [jnp.concatenate(pair) for pair in zip(near, more)]
    layer, layer_halves = scatter_first(layer, "dy")
    inputs, inputs_halves = scatter_first(inputs, "dx")
    chunk[-3] = send(chunk[-2], dz=1)
    chunk[3] = send(chunk[2], dz=-1)
    chunk[-3], chunk[3] = behind((chunk[-3], chunk[3]), *layer_halves, *inputs_halves)
    sibling[-3], sibling[3] = send(chunk[-3], flip=1), send(chunk[3], flip=1)
    layer, layer_come = scatter_second(layer, layer_halves, "dy")
    inputs, inputs_come = scatter_second(inputs, inputs_halves, "dx")
    chunk[-3], chunk[3] = behind((chunk[-3], chunk[3]), *layer_come)
    far_right, far_left = send(chunk[-3][:, :rows], dz=1), send(chunk[3][:, rows:], dz=-1)
    last = [send(far_right, flip=1), send(far_left, flip=1)]
    layer, inputs = scatter_line(layer, "dx"), scatter_line(behind(inputs, far_right, far_left), "dy")
    both = jnp.stack([layer, inputs]).astype(BF16)
    rights = jnp.stack([both[:, i] for i in (0, 2, 4, 6)], axis=1)
    lefts = jnp.stack([both[:, i] for i in (7, 1, 3, 5)], axis=1)
    away = lax.dynamic_slice_in_dim(jnp.concatenate([lefts, rights], axis=1), 3 - line, 5, 1)
    back = behind(send(away, dz=4), *last)
    result = []
    for j in range(4):
        result.append(jnp.where(line <= j, back[:, j + 1], pick(rights, jnp.minimum(j - line + 4, 3), 1)))
    for j in range(4):
        result.append(jnp.where(line >= j, back[:, j], pick(lefts, jnp.maximum(j - line - 1, 0), 1)))
    result = jnp.stack(result, axis=1).reshape(2, tokens, feats)

    second = behind(((chunk[2], chunk[-2]), (sibling[2], sibling[-2])), *inputs_halves)
    second = lax.optimization_barrier(gradients((2, -2), lay(*second)))
    pieces = behind(((chunk[3], chunk[-3]), (sibling[3], sibling[-3]), (far_right, far_left), last), away)
    third, fourth = gradients((3, -3), lay(*pieces[:2])), gradients((4,), lay(*pieces[2:]))
    totals = [(a + b + c + d).astype(BF16) for a, b, c, d in zip(early, second, third, fourth)]
    return result[0], result[1], *totals


def solution(mesh):
    return jax.shard_map(
        local,
        mesh=mesh,
        in_specs=(
            P(("depth", "col"), "row"),
            P("row", "col"),
            P("row", "col"),
            P("col", "row"),
            P(("depth", "col"), "row"),
        ),
        out_specs=(
            P(("depth", "col"), "row"),
            P(("depth", "col"), "row"),
            P(("row", "depth"), "col"),
            P(("row", "depth"), "col"),
            P("col", ("row", "depth")),
        ),
        check_vma=False,
    )
```

```python
import jax
import jax.numpy as jnp
from jax import lax
from jax.sharding import PartitionSpec as P

AXES = ("row", "col", "depth")
LAST = (((1,), (1,)), ((), ()))
FIRST = (((0,), (0,)), ((), ()))
F32 = jnp.float32
BF16 = jnp.bfloat16


def send(value, dx=0, dy=0, dz=0, flip=0):
    pairs = []
    for i in range(256):
        row, col, depth = i // 32, i // 2 % 16, i % 2
        z = (depth * 4 + row // 2 + dz) % 8
        core = row % 2 ^ flip
        y, x = (col // 4 + dy) % 4, (col % 4 + dx) % 4
        pairs.append((i, ((z % 4 * 2 + core) * 16 + y * 4 + x) * 2 + z // 4))
    return lax.ppermute(value, AXES, pairs)


def step(value, axis, by):
    return send(value, **{axis: by})


def behind(value, *done):
    return lax.optimization_barrier((value, *done))[0]


def gather_ring(value, axis):
    half = value.shape[0] // 2
    before = step(value, axis, 1)
    after = step(value, axis, -1)
    low = step(before[:half], axis, 1)
    high = step(after[half:], axis, -1)
    return [value, after, jnp.concatenate([low, high]), before]


def gather_line(value, axis):
    far = step(value, axis, 2)
    return jnp.stack([value, step(value, axis, -1), far, step(value, axis, 1)])


def scatter_first(value, axis):
    blocks = [jnp.take(value, j, axis=1 if axis == "dy" else 2) for j in range(4)]
    half = value.shape[0] // 2
    return blocks, (step(blocks[2][:half], axis, 1), step(blocks[2][half:], axis, -1))


def scatter_second(blocks, halves, axis):
    here, after, far, before = [block.astype(F32) for block in blocks]
    up, down = [half.astype(F32) for half in halves]
    half = here.shape[0] // 2
    after = jnp.concatenate([after[:half] + up, after[half:]]).astype(BF16)
    before = jnp.concatenate([before[:half], before[half:] + down]).astype(BF16)
    after, before = step(after, axis, 1), step(before, axis, -1)
    return here + after.astype(F32) + before.astype(F32), (after, before)


def scatter_line(lines, axis):
    here, after, far, before = [lines[:, j] for j in range(4)]
    total = here + step(after.astype(BF16), axis, 1).astype(F32)
    total = total + step(before.astype(BF16), axis, -1).astype(F32)
    return total + step(far.astype(BF16), axis, 2).astype(F32)


def dot(a, b, dims=(((1,), (0,)), ((), ()))):
    return lax.dot_general(a, b, dims, preferred_element_type=F32)


def half_of(value, which, axis):
    size = value.shape[axis] // 2
    return lax.dynamic_slice_in_dim(value, which * size, size, axis)


def pick(value, index, axis):
    return lax.dynamic_index_in_dim(value, index, axis, keepdims=False)


def local(activations, gate_weight, up_weight, down_weight, output_grad):
    tokens, feats = activations.shape
    units = gate_weight.shape[1]
    group = tokens // 8
    rows = 16 * group
    hu = units // 2
    row = lax.axis_index("row")
    line, core = row // 2, row % 2
    depth = lax.axis_index("depth")

    pair = jnp.stack([activations, output_grad]).reshape(2, 8, group, feats)
    foreign = send(lax.dynamic_slice_in_dim(pair[:, 1:7], line, 3, 1), dz=4)
    chosen = []
    for s in range(4):
        right = pick(pair, jnp.maximum(line - s, 0), 1)
        left = pick(pair, jnp.minimum(4 + line + s, 7), 1)
        if s > 0:
            right = jnp.where(line >= s, right, foreign[:, 3 - s])
            left = jnp.where(line + s <= 3, left, foreign[:, s - 1])
        chosen.append(jnp.stack([right, left], axis=1))
    chosen = jnp.stack(chosen, axis=1)
    lines = lax.optimization_barrier((gather_line(chosen[0], "dx"), gather_line(chosen[1], "dy")))
    act_ring = gather_ring(lines[0], "dy")
    act = jnp.stack(act_ring)
    cot = jnp.swapaxes(jnp.stack(gather_ring(lines[1], "dx")), 0, 1)
    act = jnp.transpose(act, (2, 3, 0, 1, 4, 5)).reshape(4, 2 * rows, feats)
    cot = jnp.transpose(cot, (2, 3, 0, 1, 4, 5)).reshape(4, 2 * rows, feats)

    gate_late, up_late, down_late = behind((gate_weight, up_weight, down_weight), act_ring[1])
    own_in = jnp.concatenate([half_of(gate_late, core, 1), half_of(up_late, core, 1)], axis=1)
    own_down = half_of(down_late, core, 0)
    sib_in = jnp.concatenate([half_of(gate_late, 1 - core, 1), half_of(up_late, 1 - core, 1)], axis=1)
    sib_in, sib_down = send(sib_in, flip=1), send(half_of(down_late, 1 - core, 0), flip=1)

    others = send(behind(half_of(chosen, 1 - depth, 4), lines), dz=4)
    act_sib = [send(act[0], flip=1), send(act[1:], flip=1)]
    cot_sib = [send(cot[0], flip=1), send(cot[1:], flip=1)]

    def partial(a, c, a2, c2):
        first = dot(a, own_in) + dot(a2, sib_in)
        second = dot(c, own_down, LAST) + dot(c2, sib_down, LAST)
        return jnp.concatenate([first, second], axis=1)

    sums = partial(act[0], cot[0], act_sib[0], cot_sib[0])
    message = sums.astype(BF16)
    for s in range(1, 4):
        right = send(message[:rows], dz=1)
        left = send(message[rows:], dz=-1)
        if s == 1:
            sums = partial(act[1], cot[1], act_sib[1][0], cot_sib[1][0])
            act_rest, cot_rest = behind((act[2:], cot[2:]), right, left)
        elif s == 2:
            tall = [t.reshape(4 * rows, feats) for t in (act_rest, cot_rest, act_sib[1][1:], cot_sib[1][1:])]
            rest, others = lax.optimization_barrier((partial(*tall), others))
            others = gather_line(others, "dx")
            sums = rest[: 2 * rows]
        else:
            sums = rest[2 * rows :]
        sums = sums + jnp.concatenate([right, left]).astype(F32)
        message = sums.astype(BF16)

    gate_sums, up_sums, hidden_grad = sums[:, :hu], sums[:, hu : 2 * hu], sums[:, 2 * hu :]
    sigmoid_gate = jax.nn.sigmoid(gate_sums)
    activated = gate_sums * sigmoid_gate
    hidden = (activated * up_sums).astype(BF16)
    gate_grad = (
        hidden_grad * up_sums * sigmoid_gate * (1.0 + gate_sums * (1.0 - sigmoid_gate))
    ).astype(BF16)
    up_grad = (hidden_grad * activated).astype(BF16)

    def lay(mine, theirs):
        mine, theirs = [[half for j in side for half in (j[:, : j.shape[1] // 2], j[:, j.shape[1] // 2 :])] for side in (mine, theirs)]
        mine, theirs = lax.optimization_barrier((jnp.concatenate(mine, axis=1), jnp.concatenate(theirs, axis=1)))
        return jnp.where(
            core == 0,
            jnp.concatenate([mine, theirs], axis=2),
            jnp.concatenate([theirs, mine], axis=2),
        )

    def outputs_of(whole):
        layer = dot(whole[0], down_weight)
        inputs = dot(whole[1], gate_weight, LAST) + dot(whole[2], up_weight, LAST)
        shape = (-1, 4, 4, group, feats)
        return layer.astype(BF16).reshape(shape), inputs.astype(BF16).reshape(shape)

    others = jnp.stack(gather_ring(others, "dy"))
    others = jnp.transpose(others, (2, 3, 4, 0, 1, 5, 6)).reshape(2, 4, 2, rows, feats // 2)

    hf = feats // 2
    act_half = half_of(act, depth, 2).reshape(4, 2, rows, hf)
    cot_half = half_of(cot, depth, 2).reshape(4, 2, rows, hf)

    def matching(chosen, other, keys):
        parts = []
        for j in keys:
            parts.append(chosen[3 - j, 0] if j in (0, 1, 2, 3) else other[(-1 - j) % 8, 0])
            parts.append(chosen[j + 3, 1] if j in (0, -1, -2, -3) else other[j - 1, 1])
        return jnp.concatenate(parts)

    def gradients(keys, whole):
        acts, cots = matching(act_half, others[0], keys), matching(cot_half, others[1], keys)
        return dot(acts, whole[1], FIRST), dot(acts, whole[2], FIRST), dot(whole[0], cots, FIRST)

    chunk = {0: jnp.stack([hidden, gate_grad, up_grad])}
    sibling = {}
    for j in range(1, 3):
        chunk[-j] = send(chunk[1 - j], dz=1)
        chunk[j] = send(chunk[j - 1], dz=-1)
        if j == 1:
            sibling[0] = send(chunk[0], flip=1)
        if j == 2:
            chunk[-2], chunk[2], near, early = lax.optimization_barrier((chunk[-2], chunk[2], near, early))
        sibling[-j], sibling[j] = send(chunk[-j], flip=1), send(chunk[j], flip=1)
        if j == 1:
            whole = lay([chunk[i] for i in (-1, 0, 1)], [sibling[i] for i in (-1, 0, 1)])
            near, early = outputs_of(whole), gradients((-1, 0, 1), whole)
        if j == 2:
            whole = lay((chunk[2][:, :rows], chunk[-2][:, rows:]), (sibling[2][:, :rows], sibling[-2][:, rows:]))
            more = outputs_of(whole)

    layer, inputs = [jnp.concatenate(pair) for pair in zip(near, more)]
    layer, layer_halves = scatter_first(layer, "dy")
    inputs, inputs_halves = scatter_first(inputs, "dx")
    chunk[-3] = send(chunk[-2], dz=1)
    chunk[3] = send(chunk[2], dz=-1)
    chunk[-3], chunk[3] = behind((chunk[-3], chunk[3]), *layer_halves, *inputs_halves)
    sibling[-3], sibling[3] = send(chunk[-3], flip=1), send(chunk[3], flip=1)
    layer, layer_come = scatter_second(layer, layer_halves, "dy")
    inputs, inputs_come = scatter_second(inputs, inputs_halves, "dx")
    chunk[-3], chunk[3] = behind((chunk[-3], chunk[3]), *layer_come)
    far_right, far_left = send(chunk[-3][:, :rows], dz=1), send(chunk[3][:, rows:], dz=-1)
    last = [send(far_right, flip=1), send(far_left, flip=1)]
    layer, inputs = scatter_line(layer, "dx"), scatter_line(behind(inputs, far_right, far_left), "dy")
    both = jnp.stack([layer, inputs]).astype(BF16)
    rights = jnp.stack([both[:, i] for i in (0, 2, 4, 6)], axis=1)
    lefts = jnp.stack([both[:, i] for i in (7, 1, 3, 5)], axis=1)
    away = lax.dynamic_slice_in_dim(jnp.concatenate([lefts, rights], axis=1), 3 - line, 5, 1)
    back = behind(send(away, dz=4), *last)
    result = []
    for j in range(4):
        result.append(jnp.where(line <= j, back[:, j + 1], pick(rights, jnp.minimum(j - line + 4, 3), 1)))
    for j in range(4):
        result.append(jnp.where(line >= j, back[:, j], pick(lefts, jnp.maximum(j - line - 1, 0), 1)))
    result = jnp.stack(result, axis=1).reshape(2, tokens, feats)

    second = behind(((chunk[2], chunk[-2]), (sibling[2], sibling[-2])), *inputs_halves)
    second = lax.optimization_barrier(gradients((2, -2), lay(*second)))
    pieces = behind(((chunk[3], chunk[-3]), (sibling[3], sibling[-3]), (far_right, far_left), last), away)
    third, fourth = gradients((3, -3), lay(*pieces[:2])), gradients((4,), lay(*pieces[2:]))
    totals = [(a + b + c + d).astype(BF16) for a, b, c, d in zip(early, second, third, fourth)]
    return result[0], result[1], *totals


def solution(mesh):
    return jax.shard_map(
        local,
        mesh=mesh,
        in_specs=(
            P(("depth", "col"), "row"),
            P("row", "col"),
            P("row", "col"),
            P("col", "row"),
            P(("depth", "col"), "row"),
        ),
        out_specs=(
            P(("depth", "col"), "row"),
            P(("depth", "col"), "row"),
            P(("row", "depth"), "col"),
            P(("row", "depth"), "col"),
            P("col", ("row", "depth")),
        ),
        check_vma=False,
    )
```

```python
import jax
import jax.numpy as jnp
from jax import lax
from jax.sharding import PartitionSpec as P

AXES = ("row", "col", "depth")
LAST = (((1,), (1,)), ((), ()))
FIRST = (((0,), (0,)), ((), ()))
F32 = jnp.float32
BF16 = jnp.bfloat16


def send(value, dx=0, dy=0, dz=0, flip=0):
    pairs = []
    for i in range(256):
        row, col, depth = i // 32, i // 2 % 16, i % 2
        z = (depth * 4 + row // 2 + dz) % 8
        core = row % 2 ^ flip
        y, x = (col // 4 + dy) % 4, (col % 4 + dx) % 4
        pairs.append((i, ((z % 4 * 2 + core) * 16 + y * 4 + x) * 2 + z // 4))
    return lax.ppermute(value, AXES, pairs)


def step(value, axis, by):
    return send(value, **{axis: by})


def behind(value, *done):
    return lax.optimization_barrier((value, *done))[0]


def gather_ring(value, axis):
    half = value.shape[0] // 2
    before = step(value, axis, 1)
    after = step(value, axis, -1)
    low = step(before[:half], axis, 1)
    high = step(after[half:], axis, -1)
    return [value, after, jnp.concatenate([low, high]), before]


def gather_line(value, axis):
    far = step(value, axis, 2)
    return jnp.stack([value, step(value, axis, -1), far, step(value, axis, 1)])


def scatter_first(value, axis):
    blocks = [jnp.take(value, j, axis=1 if axis == "dy" else 2) for j in range(4)]
    half = value.shape[0] // 2
    return blocks, (step(blocks[2][:half], axis, 1), step(blocks[2][half:], axis, -1))


def scatter_second(blocks, halves, axis):
    here, after, far, before = [block.astype(F32) for block in blocks]
    up, down = [half.astype(F32) for half in halves]
    half = here.shape[0] // 2
    after = jnp.concatenate([after[:half] + up, after[half:]]).astype(BF16)
    before = jnp.concatenate([before[:half], before[half:] + down]).astype(BF16)
    after, before = step(after, axis, 1), step(before, axis, -1)
    return here + after.astype(F32) + before.astype(F32), (after, before)


def scatter_line(lines, axis):
    here, after, far, before = [lines[:, j] for j in range(4)]
    total = here + step(after.astype(BF16), axis, 1).astype(F32)
    total = total + step(before.astype(BF16), axis, -1).astype(F32)
    return total + step(far.astype(BF16), axis, 2).astype(F32)


def dot(a, b, dims=(((1,), (0,)), ((), ()))):
    return lax.dot_general(a, b, dims, preferred_element_type=F32)


def half_of(value, which, axis):
    size = value.shape[axis] // 2
    return lax.dynamic_slice_in_dim(value, which * size, size, axis)


def pick(value, index, axis):
    return lax.dynamic_index_in_dim(value, index, axis, keepdims=False)


def local(activations, gate_weight, up_weight, down_weight, output_grad):
    tokens, feats = activations.shape
    units = gate_weight.shape[1]
    group = tokens // 8
    rows = 16 * group
    hu = units // 2
    row = lax.axis_index("row")
    line, core = row // 2, row % 2
    depth = lax.axis_index("depth")

    pair = jnp.stack([activations, output_grad]).reshape(2, 8, group, feats)
    foreign = send(lax.dynamic_slice_in_dim(pair[:, 1:7], line, 3, 1), dz=4)
    chosen = []
    for s in range(4):
        right = pick(pair, jnp.maximum(line - s, 0), 1)
        left = pick(pair, jnp.minimum(4 + line + s, 7), 1)
        if s > 0:
            right = jnp.where(line >= s, right, foreign[:, 3 - s])
            left = jnp.where(line + s <= 3, left, foreign[:, s - 1])
        chosen.append(jnp.stack([right, left], axis=1))
    chosen = jnp.stack(chosen, axis=1)
    lines = lax.optimization_barrier((gather_line(chosen[1], "dy"), gather_line(chosen[0], "dx")))
    cot = jnp.swapaxes(jnp.stack(gather_ring(lines[0], "dx")), 0, 1)
    act_ring = gather_ring(lines[1], "dy")
    act = jnp.stack(act_ring)
    act = jnp.transpose(act, (2, 3, 0, 1, 4, 5)).reshape(4, 2 * rows, feats)
    cot = jnp.transpose(cot, (2, 3, 0, 1, 4, 5)).reshape(4, 2 * rows, feats)

    gate_late, up_late, down_late = behind((gate_weight, up_weight, down_weight), act_ring[1])
    own_in = jnp.concatenate([half_of(gate_late, core, 1), half_of(up_late, core, 1)], axis=1)
    own_down = half_of(down_late, core, 0)
    sib_in = jnp.concatenate([half_of(gate_late, 1 - core, 1), half_of(up_late, 1 - core, 1)], axis=1)
    sib_in, sib_down = send(sib_in, flip=1), send(half_of(down_late, 1 - core, 0), flip=1)

    others = send(behind(half_of(chosen, 1 - depth, 4), lines), dz=4)
    act_sib = [send(act[0], flip=1), send(act[1:], flip=1)]
    cot_sib = [send(cot[0], flip=1), send(cot[1:], flip=1)]

    def partial(a, c, a2, c2):
        first = dot(a, own_in) + dot(a2, sib_in)
        second = dot(c, own_down, LAST) + dot(c2, sib_down, LAST)
        return jnp.concatenate([first, second], axis=1)

    sums = partial(act[0], cot[0], act_sib[0], cot_sib[0])
    message = sums.astype(BF16)
    act_rest, cot_rest = act[1:], cot[1:]
    for s in range(1, 4):
        right = send(message[:rows], dz=1)
        left = send(message[rows:], dz=-1)
        if s == 1:
            act_late, cot_late = behind((act_rest, cot_rest), right, left)
        else:
            act_rest, cot_rest = act_late, cot_late
        sums = partial(act_rest[s - 1], cot_rest[s - 1], act_sib[1][s - 1], cot_sib[1][s - 1])
        if s == 2:
            sums, others = lax.optimization_barrier((sums, others))
        sums = sums + jnp.concatenate([right, left]).astype(F32)
        message = sums.astype(BF16)

    gate_sums, up_sums, hidden_grad = sums[:, :hu], sums[:, hu : 2 * hu], sums[:, 2 * hu :]
    sigmoid_gate = jax.nn.sigmoid(gate_sums)
    activated = gate_sums * sigmoid_gate
    hidden = (activated * up_sums).astype(BF16)
    gate_grad = (
        hidden_grad * up_sums * sigmoid_gate * (1.0 + gate_sums * (1.0 - sigmoid_gate))
    ).astype(BF16)
    up_grad = (hidden_grad * activated).astype(BF16)

    def lay(mine, theirs):
        mine, theirs = [[half for j in side for half in (j[:, : j.shape[1] // 2], j[:, j.shape[1] // 2 :])] for side in (mine, theirs)]
        mine, theirs = lax.optimization_barrier((jnp.concatenate(mine, axis=1), jnp.concatenate(theirs, axis=1)))
        return jnp.where(
            core == 0,
            jnp.concatenate([mine, theirs], axis=2),
            jnp.concatenate([theirs, mine], axis=2),
        )

    def outputs_of(whole):
        layer = dot(whole[0], down_weight)
        inputs = dot(whole[1], gate_weight, LAST) + dot(whole[2], up_weight, LAST)
        shape = (-1, 4, 4, group, feats)
        return layer.astype(BF16).reshape(shape), inputs.astype(BF16).reshape(shape)

    chunk = {0: jnp.stack([hidden, gate_grad, up_grad])}
    sibling = {}
    for j in range(1, 3):
        chunk[-j] = send(chunk[1 - j], dz=1)
        chunk[j] = send(chunk[j - 1], dz=-1)
        if j == 1:
            sibling[0] = send(chunk[0], flip=1)
            lines = gather_line(behind(others, sibling[0]), "dx")
            chunk_near = behind((chunk[-1], chunk[1]), lines)
        if j == 2:
            others = jnp.stack(gather_ring(behind(lines, sibling[-1], sibling[1]), "dy"))
            others = jnp.transpose(others, (2, 3, 4, 0, 1, 5, 6)).reshape(2, 4, 2, rows, feats // 2)
            chunk[-2], chunk[2], near, others = lax.optimization_barrier((chunk[-2], chunk[2], near, others))
        before, after = chunk_near if j == 1 else (chunk[-2], chunk[2])
        sibling[-j], sibling[j] = send(before, flip=1), send(after, flip=1)
        if j == 1:
            whole = lay([chunk[i] for i in (-1, 0, 1)], [sibling[i] for i in (-1, 0, 1)])
            near, near_whole = outputs_of(whole), whole
        if j == 2:
            whole = lay((chunk[2][:, :rows], chunk[-2][:, rows:]), (sibling[2][:, :rows], sibling[-2][:, rows:]))
            more = outputs_of(whole)

    layer, inputs = [jnp.concatenate(pair) for pair in zip(near, more)]
    layer, layer_halves = scatter_first(layer, "dy")
    inputs, inputs_halves = scatter_first(inputs, "dx")
    chunk[-3] = send(chunk[-2], dz=1)
    chunk[3] = send(chunk[2], dz=-1)
    chunk[-3], chunk[3] = behind((chunk[-3], chunk[3]), *layer_halves, *inputs_halves)
    sibling[-3], sibling[3] = send(chunk[-3], flip=1), send(chunk[3], flip=1)
    layer, layer_come = scatter_second(layer, layer_halves, "dy")
    inputs, inputs_come = scatter_second(inputs, inputs_halves, "dx")
    chunk[-3], chunk[3] = behind((chunk[-3], chunk[3]), *layer_come)
    far_right, far_left = send(chunk[-3][:, :rows], dz=1), send(chunk[3][:, rows:], dz=-1)
    last = [send(far_right, flip=1), send(far_left, flip=1)]
    layer, inputs = scatter_line(layer, "dx"), scatter_line(behind(inputs, far_right, far_left), "dy")
    both = jnp.stack([layer, inputs]).astype(BF16)
    rights = jnp.stack([both[:, i] for i in (0, 2, 4, 6)], axis=1)
    lefts = jnp.stack([both[:, i] for i in (7, 1, 3, 5)], axis=1)
    away = lax.dynamic_slice_in_dim(jnp.concatenate([lefts, rights], axis=1), 3 - line, 5, 1)
    back = behind(send(away, dz=4), *last)
    result = []
    for j in range(4):
        result.append(jnp.where(line <= j, back[:, j + 1], pick(rights, jnp.minimum(j - line + 4, 3), 1)))
    for j in range(4):
        result.append(jnp.where(line >= j, back[:, j], pick(lefts, jnp.maximum(j - line - 1, 0), 1)))
    result = jnp.stack(result, axis=1).reshape(2, tokens, feats)

    hf = feats // 2
    act_half = half_of(act, depth, 2).reshape(4, 2, rows, hf)
    cot_half = half_of(cot, depth, 2).reshape(4, 2, rows, hf)

    def matching(chosen, other, keys):
        parts = []
        for j in keys:
            parts.append(chosen[3 - j, 0] if j in (0, 1, 2, 3) else other[(-1 - j) % 8, 0])
            parts.append(chosen[j + 3, 1] if j in (0, -1, -2, -3) else other[j - 1, 1])
        return jnp.concatenate(parts)

    def gradients(keys, whole):
        acts, cots = matching(act_half, others[0], keys), matching(cot_half, others[1], keys)
        return dot(acts, whole[1], FIRST), dot(acts, whole[2], FIRST), dot(whole[0], cots, FIRST)

    early = lax.optimization_barrier(gradients((-1, 0, 1), behind(near_whole, *inputs_halves)))
    second = behind(((chunk[2], chunk[-2]), (sibling[2], sibling[-2])), *inputs_halves)
    second = lax.optimization_barrier(gradients((2, -2), lay(*second)))
    pieces = behind(((chunk[3], chunk[-3]), (sibling[3], sibling[-3]), (far_right, far_left), last), away)
    third, fourth = gradients((3, -3), lay(*pieces[:2])), gradients((4,), lay(*pieces[2:]))
    totals = [(a + b + c + d).astype(BF16) for a, b, c, d in zip(early, second, third, fourth)]
    return result[0], result[1], *totals


def solution(mesh):
    return jax.shard_map(
        local,
        mesh=mesh,
        in_specs=(
            P(("depth", "col"), "row"),
            P("row", "col"),
            P("row", "col"),
            P("col", "row"),
            P(("depth", "col"), "row"),
        ),
        out_specs=(
            P(("depth", "col"), "row"),
            P(("depth", "col"), "row"),
            P(("row", "depth"), "col"),
            P(("row", "depth"), "col"),
            P("col", ("row", "depth")),
        ),
        check_vma=False,
    )
```

```python
import jax
import jax.numpy as jnp
from jax import lax
from jax.sharding import PartitionSpec as P

AXES = ("row", "col", "depth")
LAST = (((1,), (1,)), ((), ()))
FIRST = (((0,), (0,)), ((), ()))
F32 = jnp.float32
BF16 = jnp.bfloat16


def send(value, dx=0, dy=0, dz=0, flip=0):
    pairs = []
    for i in range(256):
        row, col, depth = i // 32, i // 2 % 16, i % 2
        z = (depth * 4 + row // 2 + dz) % 8
        core = row % 2 ^ flip
        y, x = (col // 4 + dy) % 4, (col % 4 + dx) % 4
        pairs.append((i, ((z % 4 * 2 + core) * 16 + y * 4 + x) * 2 + z // 4))
    return lax.ppermute(value, AXES, pairs)


def step(value, axis, by):
    return send(value, **{axis: by})


def behind(value, *done):
    return lax.optimization_barrier((value, *done))[0]


def gather_ring(value, axis, neighbours=None, done=()):
    half = value.shape[0] // 2
    before, after = neighbours or (step(value, axis, 1), step(value, axis, -1))
    low, high = behind((before[:half], after[half:]), *done)
    low, high = step(low, axis, 1), step(high, axis, -1)
    return [value, after, jnp.concatenate([low, high]), before]


def gather_line(value, axis):
    far = step(value, axis, 2)
    return jnp.stack([value, step(value, axis, -1), far, step(value, axis, 1)])


def scatter_first(value, axis):
    blocks = [jnp.take(value, j, axis=1 if axis == "dy" else 2) for j in range(4)]
    half = value.shape[0] // 2
    return blocks, (step(blocks[2][:half], axis, 1), step(blocks[2][half:], axis, -1))


def scatter_second(blocks, halves, axis):
    here, after, far, before = [block.astype(F32) for block in blocks]
    up, down = [half.astype(F32) for half in halves]
    half = here.shape[0] // 2
    after = jnp.concatenate([after[:half] + up, after[half:]]).astype(BF16)
    before = jnp.concatenate([before[:half], before[half:] + down]).astype(BF16)
    after, before = step(after, axis, 1), step(before, axis, -1)
    return here + after.astype(F32) + before.astype(F32), (after, before)


def scatter_line(lines, axis):
    here, after, far, before = [lines[:, j] for j in range(4)]
    total = here + step(after.astype(BF16), axis, 1).astype(F32)
    total = total + step(before.astype(BF16), axis, -1).astype(F32)
    return total + step(far.astype(BF16), axis, 2).astype(F32)


def dot(a, b, dims=(((1,), (0,)), ((), ()))):
    return lax.dot_general(a, b, dims, preferred_element_type=F32)


def half_of(value, which, axis):
    size = value.shape[axis] // 2
    return lax.dynamic_slice_in_dim(value, which * size, size, axis)


def pick(value, index, axis):
    return lax.dynamic_index_in_dim(value, index, axis, keepdims=False)


def local(activations, gate_weight, up_weight, down_weight, output_grad):
    tokens, feats = activations.shape
    units = gate_weight.shape[1]
    group = tokens // 8
    rows = 16 * group
    hu = units // 2
    row = lax.axis_index("row")
    line, core = row // 2, row % 2
    depth = lax.axis_index("depth")

    pair = jnp.stack([activations, output_grad]).reshape(2, 8, group, feats)
    foreign = send(lax.dynamic_slice_in_dim(pair[:, 1:7], line, 3, 1), dz=4)
    chosen = []
    for s in range(4):
        right = pick(pair, jnp.maximum(line - s, 0), 1)
        left = pick(pair, jnp.minimum(4 + line + s, 7), 1)
        if s > 0:
            right = jnp.where(line >= s, right, foreign[:, 3 - s])
            left = jnp.where(line + s <= 3, left, foreign[:, s - 1])
        chosen.append(jnp.stack([right, left], axis=1))
    chosen = jnp.stack(chosen, axis=1)
    lines = lax.optimization_barrier((gather_line(chosen[1], "dy"), gather_line(chosen[0], "dx")))
    cot = jnp.swapaxes(jnp.stack(gather_ring(lines[0], "dx")), 0, 1)
    act_ring = gather_ring(lines[1], "dy")
    act = jnp.stack(act_ring)
    act = jnp.transpose(act, (2, 3, 0, 1, 4, 5)).reshape(4, 2 * rows, feats)
    cot = jnp.transpose(cot, (2, 3, 0, 1, 4, 5)).reshape(4, 2 * rows, feats)

    gate_late, up_late, down_late = behind((gate_weight, up_weight, down_weight), act_ring[1])
    own_in = jnp.concatenate([half_of(gate_late, core, 1), half_of(up_late, core, 1)], axis=1)
    own_down = half_of(down_late, core, 0)
    sib_in = jnp.concatenate([half_of(gate_late, 1 - core, 1), half_of(up_late, 1 - core, 1)], axis=1)
    sib_in, sib_down = send(sib_in, flip=1), send(half_of(down_late, 1 - core, 0), flip=1)

    others = send(behind(half_of(chosen, 1 - depth, 4), lines), dz=4)
    act_sib = [send(act[0], flip=1), send(act[1:], flip=1)]
    cot_sib = [send(cot[0], flip=1), send(cot[1:], flip=1)]

    def partial(a, c, a2, c2):
        first = dot(a, own_in) + dot(a2, sib_in)
        second = dot(c, own_down, LAST) + dot(c2, sib_down, LAST)
        return jnp.concatenate([first, second], axis=1)

    sums = partial(act[0], cot[0], act_sib[0], cot_sib[0])
    message = sums.astype(BF16)
    act_rest, cot_rest = act[1:], cot[1:]
    for s in range(1, 4):
        right = send(message[:rows], dz=1)
        left = send(message[rows:], dz=-1)
        if s == 1:
            act_late, cot_late = behind((act_rest, cot_rest), right, left)
        elif s == 3:
            act_rest, cot_rest = act_late, cot_late
        sums = partial(act_rest[s - 1], cot_rest[s - 1], act_sib[1][s - 1], cot_sib[1][s - 1])
        if s == 2:
            sums, others = lax.optimization_barrier((sums, others))
        sums = sums + jnp.concatenate([right, left]).astype(F32)
        message = sums.astype(BF16)

    gate_sums, up_sums, hidden_grad = sums[:, :hu], sums[:, hu : 2 * hu], sums[:, 2 * hu :]
    sigmoid_gate = jax.nn.sigmoid(gate_sums)
    activated = gate_sums * sigmoid_gate
    hidden = (activated * up_sums).astype(BF16)
    gate_grad = (
        hidden_grad * up_sums * sigmoid_gate * (1.0 + gate_sums * (1.0 - sigmoid_gate))
    ).astype(BF16)
    up_grad = (hidden_grad * activated).astype(BF16)

    def lay(mine, theirs):
        mine, theirs = [[half for j in side for half in (j[:, : j.shape[1] // 2], j[:, j.shape[1] // 2 :])] for side in (mine, theirs)]
        mine, theirs = lax.optimization_barrier((jnp.concatenate(mine, axis=1), jnp.concatenate(theirs, axis=1)))
        return jnp.where(
            core == 0,
            jnp.concatenate([mine, theirs], axis=2),
            jnp.concatenate([theirs, mine], axis=2),
        )

    def outputs_of(whole):
        layer = dot(whole[0], down_weight)
        inputs = dot(whole[1], gate_weight, LAST) + dot(whole[2], up_weight, LAST)
        shape = (-1, 4, 4, group, feats)
        return layer.astype(BF16).reshape(shape), inputs.astype(BF16).reshape(shape)

    chunk = {0: jnp.stack([hidden, gate_grad, up_grad])}
    sibling = {}
    for j in range(1, 3):
        chunk[-j] = send(chunk[1 - j], dz=1)
        chunk[j] = send(chunk[j - 1], dz=-1)
        if j == 1:
            sibling[0] = send(chunk[0], flip=1)
            lines = gather_line(behind(others, sibling[0]), "dx")
            chunk_near = behind((chunk[-1], chunk[1]), lines)
        if j == 2:
            come = behind(lines, sibling[-1], sibling[1])
            come = step(come, "dy", 1), step(come, "dy", -1)
            chunk[-2], chunk[2], near, come = lax.optimization_barrier((chunk[-2], chunk[2], near, come))
        before, after = chunk_near if j == 1 else (chunk[-2], chunk[2])
        sibling[-j], sibling[j] = send(before, flip=1), send(after, flip=1)
        if j == 1:
            whole = lay([chunk[i] for i in (-1, 0, 1)], [sibling[i] for i in (-1, 0, 1)])
            near, near_whole = outputs_of(whole), whole
        if j == 2:
            whole = lay((chunk[2][:, :rows], chunk[-2][:, rows:]), (sibling[2][:, :rows], sibling[-2][:, rows:]))
            more = outputs_of(whole)

    layer, inputs = [jnp.concatenate(pair) for pair in zip(near, more)]
    layer, layer_halves = scatter_first(layer, "dy")
    inputs, inputs_halves = scatter_first(inputs, "dx")
    others = jnp.stack(gather_ring(lines, "dy", come, layer_halves))
    others = jnp.transpose(others, (2, 3, 4, 0, 1, 5, 6)).reshape(2, 4, 2, rows, feats // 2)
    chunk[-3] = send(chunk[-2], dz=1)
    chunk[3] = send(chunk[2], dz=-1)
    chunk[-3], chunk[3] = behind((chunk[-3], chunk[3]), *layer_halves, *inputs_halves)
    sibling[-3], sibling[3] = send(chunk[-3], flip=1), send(chunk[3], flip=1)
    layer, layer_come = scatter_second(layer, layer_halves, "dy")
    inputs, inputs_come = scatter_second(inputs, inputs_halves, "dx")
    chunk[-3], chunk[3] = behind((chunk[-3], chunk[3]), *layer_come)
    far_right, far_left = send(chunk[-3][:, :rows], dz=1), send(chunk[3][:, rows:], dz=-1)
    last = [send(far_right, flip=1), send(far_left, flip=1)]
    layer, inputs = scatter_line(layer, "dx"), scatter_line(behind(inputs, far_right, far_left), "dy")
    both = jnp.stack([layer, inputs]).astype(BF16)
    rights = jnp.stack([both[:, i] for i in (0, 2, 4, 6)], axis=1)
    lefts = jnp.stack([both[:, i] for i in (7, 1, 3, 5)], axis=1)
    away = lax.dynamic_slice_in_dim(jnp.concatenate([lefts, rights], axis=1), 3 - line, 5, 1)
    back = behind(send(away, dz=4), *last)
    result = []
    for j in range(4):
        result.append(jnp.where(line <= j, back[:, j + 1], pick(rights, jnp.minimum(j - line + 4, 3), 1)))
    for j in range(4):
        result.append(jnp.where(line >= j, back[:, j], pick(lefts, jnp.maximum(j - line - 1, 0), 1)))
    result = jnp.stack(result, axis=1).reshape(2, tokens, feats)

    hf = feats // 2
    act_half = half_of(act, depth, 2).reshape(4, 2, rows, hf)
    cot_half = half_of(cot, depth, 2).reshape(4, 2, rows, hf)

    def matching(chosen, other, keys):
        parts = []
        for j in keys:
            parts.append(chosen[3 - j, 0] if j in (0, 1, 2, 3) else other[(-1 - j) % 8, 0])
            parts.append(chosen[j + 3, 1] if j in (0, -1, -2, -3) else other[j - 1, 1])
        return jnp.concatenate(parts)

    def gradients(keys, whole):
        acts, cots = matching(act_half, others[0], keys), matching(cot_half, others[1], keys)
        return dot(acts, whole[1], FIRST), dot(acts, whole[2], FIRST), dot(whole[0], cots, FIRST)

    early = lax.optimization_barrier(gradients((-1, 0, 1), behind(near_whole, *inputs_halves)))
    second = behind(((chunk[2], chunk[-2]), (sibling[2], sibling[-2])), *inputs_halves)
    second = lax.optimization_barrier(gradients((2, -2), lay(*second)))
    pieces = behind(((chunk[3], chunk[-3]), (sibling[3], sibling[-3]), (far_right, far_left), last), away)
    third, fourth = gradients((3, -3), lay(*pieces[:2])), gradients((4,), lay(*pieces[2:]))
    totals = [(a + b + c + d).astype(BF16) for a, b, c, d in zip(early, second, third, fourth)]
    return result[0], result[1], *totals


def solution(mesh):
    return jax.shard_map(
        local,
        mesh=mesh,
        in_specs=(
            P(("depth", "col"), "row"),
            P("row", "col"),
            P("row", "col"),
            P("col", "row"),
            P(("depth", "col"), "row"),
        ),
        out_specs=(
            P(("depth", "col"), "row"),
            P(("depth", "col"), "row"),
            P(("row", "depth"), "col"),
            P(("row", "depth"), "col"),
            P("col", ("row", "depth")),
        ),
        check_vma=False,
    )
```
